128 devices in a mesh: ping: 8 (over y, x_hi), range: 8 (over z, x_lo), elev: 2 (over core).
Axes of the slice: x: 4 (x_hi: 2, x_lo: 2; x = x_hi * 2 + x_lo), y: 4, z: 4, core: 2. Of those that a mesh axis runs over, the one named last changes fastest.
Arguments:
- echoes: bfloat16 [32, 16, 64, 1024], P('ping', 'elev', None, 'range'), may hold values from -6 to 6
- steer: bfloat16 [16, 8, 1024], P('elev', None, 'range'), may hold values from -1.5 to 1.5
- offsets: int32 [32], P('ping'), may hold values from 0 to 64, as said below
- delays: int32 [32, 256], P('ping'), may hold values from 0 to 7
- aperture: int32 [128, 32], P(None, 'ping'), may hold values 0 or 1
Outputs:
- image: bfloat16 [128, 8, 1024], P(('ping', 'elev'), None, 'range')
The draws below stay inside these ranges and needn't reach their ends.
Inputs may be any that keep to these rules, and one draw needn't show every extreme that they name: offsets[p] + 64 <= 128, so every element of every ping lies on a voxel column.
All inputs are finite; a program needn't handle non-finite values. No bound on the sum of `aperture` on one device may be relied on, other than what follows from the above.
Results may differ from the reference program's by a relative error of at most 0.0049.
Values may be sent and summed in bfloat16 or wider, within the bound.
A program may use at most 64 MiB of HBM per device.

```python
import jax
import jax.numpy as jnp
from jax import lax

ELEV = 16
ALONG = 64
HALVES = 2
BEAMS = 8
DMAX = 8
PINGS = 32
NR = 1024
NX = 128


def draw_offsets(key, part):
    key = jax.random.fold_in(key, 11)
    room = NX - ALONG
    ping_ids = jnp.arange(PINGS, dtype=jnp.int32)
    base = ping_ids * room // (PINGS - 1)
    jitter = jax.random.randint(key, (PINGS,), -6, 7)
    placed = jnp.clip(base + jitter, 0, room)
    placed = placed.at[0].set(0).at[PINGS - 1].set(room)
    return placed.astype(jnp.int32)


def touch_ends(values, own_key, smallest, largest):
    spot = [jax.random.randint(jax.random.fold_in(own_key, axis), (), 0, length) for axis, length in enumerate(values.shape)]
    widest = values.shape.index(max(values.shape))
    neighbour = spot[:widest] + [(spot[widest] + 1) % values.shape[widest]] + spot[widest + 1:]
    return values.at[tuple(spot)].set(smallest).at[tuple(neighbour)].set(largest)


def steps_of(key, dims, cuts, low, top_value):
    loudness = 1.0
    for position, parts in cuts:
        steps = jax.random.uniform(jax.random.fold_in(jax.random.fold_in(key, 6), position), (parts,), jnp.float32, low / len(cuts), top_value / len(cuts))
        loudness = loudness * jnp.repeat(jnp.exp(steps), dims[position] // parts).reshape((-1,) + (1,) * (len(dims) - 1 - position))
    return loudness


def centred(own_key, shape, width, reach, split=(), kind=jnp.bfloat16):
    values = width * jax.random.normal(own_key, shape, jnp.float32)
    if split:
        values = values * steps_of(own_key, shape, split, -0.22, 0.18)
    return jnp.clip(values, -reach, reach).astype(kind)


def setup_inputs(seed: int = 0) -> dict:
    arg_keys = jax.random.split(jax.random.key(seed), 6)
    return {
        "echoes": centred(arg_keys[0], (PINGS, ELEV, ALONG, NR), 1.0, 6.0, ((0, 8), (1, 2), (3, 8))),
        "steer": centred(arg_keys[1], (ELEV, BEAMS, NR), ELEV ** -0.5, 1.5, ((0, 2), (2, 8))),
        "offsets": draw_offsets(jax.random.fold_in(arg_keys[5], 71), 0),
        "delays": touch_ends(jax.random.randint(arg_keys[3], (PINGS, 2 * NX), 0, DMAX), jax.random.fold_in(arg_keys[3], 1), 0, DMAX - 1).astype(jnp.int32),
        "aperture": touch_ends((jax.random.randint(arg_keys[4], (NX, PINGS), 0, 2) < 1).astype(jnp.int32), jax.random.fold_in(arg_keys[4], 1), 0, 1),
    }


def reference(echoes, steer, offsets, delays, aperture):
    elems_half = ELEV // HALVES
    along_iota = jnp.arange(ALONG, dtype=jnp.int32)
    column_iota = jnp.arange(NX, dtype=jnp.int32)
    delay_iota = jnp.arange(DMAX, dtype=jnp.int32)
    echo_halves = echoes.reshape(PINGS, HALVES, elems_half, ALONG, NR)
    steer_halves = steer.reshape(HALVES, elems_half, BEAMS, NR).astype(jnp.float32)
    valid_rows = jnp.transpose(aperture)

    def one_ping(total, inputs):
        echo_ping, offset, table, valid = inputs
        partial_value = jnp.einsum("hear,hebr->habr", echo_ping.astype(jnp.float32), steer_halves)
        partial_value = partial_value.astype(jnp.bfloat16)
        padded = jnp.pad(partial_value, ((0, 0), (0, 0), (0, 0), (0, DMAX - 1)))
        stacked = jnp.stack([padded[..., shift:shift + NR] for shift in range(DMAX)], axis=2)
        index = (column_iota[:, None] - offset - along_iota[None, :] + NX).astype(jnp.int32)
        picked = table[index]
        onehot = picked[:, :, None] == delay_iota[None, None, :]
        weight = jnp.where(onehot, valid[:, None, None], 0).astype(jnp.float32)
        weight = weight.reshape(NX, ALONG * DMAX)
        for half in range(HALVES):
            rows = stacked[half].reshape(ALONG * DMAX, BEAMS * NR).astype(jnp.float32)
            total = total + jnp.dot(weight, rows, precision=lax.Precision.HIGHEST)
        return total, None

    start = jnp.zeros((NX, BEAMS * NR), jnp.float32)
    total, _ = lax.scan(one_ping, start, (echo_halves, offsets, delays, valid_rows))
    scale = float(PINGS * ALONG) ** -0.5
    return (total * scale).reshape(NX, BEAMS, NR).astype(jnp.bfloat16)
```

```python
import functools

import jax
import jax.numpy as jnp
from jax import lax
from jax.experimental import pallas as pl
from jax.experimental.pallas import tpu as pltpu
from jax.sharding import PartitionSpec as P

MESH = pl.DeviceIdType.MESH
DMAX = 8
F32 = jnp.float32
BF16 = jnp.bfloat16

ROUTES = ((2, 1), (2, 0), (1, 1), (3, 1), (1, 0), (3, 0), (0, 1), (0, 0))


def target_of(ping, route):
    steps, flip = route
    y, far = ping // 2, ping % 2
    return ((y + steps) % 4) * 2 + (far + flip) % 2


def lanes(shape):
    return lax.broadcasted_iota(jnp.int32, shape, len(shape) - 1)


def rows_of(shape):
    return lax.broadcasted_iota(jnp.int32, shape, len(shape) - 2)


def kernel(
    scale, groups,
    echo_hbm, steer_hbm, off_hbm, delay_hbm, ap_hbm, out_ref,
    echo, steer, off, delay, ap, spread, wide, table, weight, pick_t,
    head, halo, give, own, sib, halo_rows, stage, got,
    in_sem, small_sem, halo_send, halo_recv, sib_send, sib_recv, share_send, share_recv,
):
    ping = lax.axis_index("ping")
    rng = lax.axis_index("range")
    elev = lax.axis_index("elev")
    other = 1 - elev
    pings, elems, along, bins = echo.shape
    half = steer.shape[1] // 2
    depth = pings * along

    loads = [
        pltpu.make_async_copy(src, dst, small_sem.at[i])
        for i, (src, dst) in enumerate(
            ((steer_hbm, steer), (off_hbm, off), (delay_hbm, delay), (ap_hbm, ap))
        )
    ]
    for load in loads:
        load.start()
    echo_loads = [
        pltpu.make_async_copy(echo_hbm.at[p], echo.at[p], in_sem.at[p]) for p in range(pings)
    ]
    for load in echo_loads:
        load.start()

    below = (rng + groups - 1) % groups
    above = (rng + 1) % groups
    barrier = pltpu.get_barrier_semaphore()
    peers = []
    for route in ROUTES:
        for side in (other, elev):
            if route != (0, 0) or side is other:
                peers.append({"ping": target_of(ping, route), "elev": side})
    for group in (below, above):
        for side in (0, 1):
            peers.append({"range": group, "elev": jnp.int32(side)})
    for peer in peers:
        pl.semaphore_signal(barrier, inc=1, device_id=peer, device_id_type=MESH)

    loads[0].wait()
    wide[...] = jnp.zeros_like(wide)
    low = lanes((8, bins)) == rows_of((8, bins))
    for e in range(elems):
        rows = steer[e].astype(F32)
        for c in range(2):
            diag = jnp.zeros((8, bins), F32)
            for b in range(half):
                beam = c * half + b
                line = jnp.broadcast_to(rows[beam : beam + 1], (8, bins))
                spread[beam, e] = line
                part = jnp.where(low, line, 0.0)
                diag = diag + (pltpu.roll(part, 8 * b, 1) if b else part)
            diag = diag + pltpu.roll(diag, 32, 1)
            diag = diag + pltpu.roll(diag, 64, 1)
            both = jnp.concatenate([diag, jnp.zeros_like(diag)], axis=0).astype(BF16)
            wide[pl.ds(e * bins, 16), pl.ds(c * bins, bins)] = both

    for load in echo_loads:
        load.wait()
    lhs = jnp.concatenate(
        [jnp.concatenate([echo[p, e] for e in range(elems)], axis=1) for p in range(pings)], axis=0
    )
    first = jnp.dot(lhs, wide[...], preferred_element_type=F32)
    place = (lanes((along, 2 * bins)) // 32) % 4
    packed = first[:along]
    for p in range(1, pings):
        packed = jnp.where(place == p, first[p * along : (p + 1) * along], packed)
    packed = packed.astype(BF16)
    for c in range(2):
        head[c] = packed[:, c * bins : (c + 1) * bins]

    pl.semaphore_wait(barrier, len(peers))

    halo_copies = []
    for c in range(2):
        copy = pltpu.make_async_remote_copy(
            src_ref=head.at[c],
            dst_ref=halo.at[elev],
            send_sem=halo_send.at[c],
            recv_sem=halo_recv.at[elev],
            device_id={"range": below, "elev": jnp.int32(c)},
            device_id_type=MESH,
        )
        copy.start()
        halo_copies.append(copy)

    def beams(p, side, dst):
        def tile(i, carry):
            start = pl.multiple_of(i * 16, 16)
            values = [echo[p, e, pl.ds(start, 16), :].astype(F32) for e in range(elems)]
            for b in range(half):
                total = None
                for e in range(elems):
                    line = spread[side * half + b, e]
                    term = values[e] * jnp.concatenate([line, line], axis=0)
                    total = term if total is None else total + term
                dst[p, pl.ds(start, 16), pl.ds(b * bins, bins)] = total.astype(BF16)
            return carry

        lax.fori_loop(0, along // 16, tile, 0)

    sib_copies = []
    for p in range(pings):
        beams(p, other, give)
        copy = pltpu.make_async_remote_copy(
            src_ref=give.at[p],
            dst_ref=sib.at[p],
            send_sem=sib_send.at[p],
            recv_sem=sib_recv.at[p],
            device_id={"elev": other},
            device_id_type=MESH,
        )
        copy.start()
        sib_copies.append(copy)
    for p in range(pings):
        beams(p, elev, own)

    for load in loads[1:]:
        load.wait()
    for p in range(pings):
        line = jnp.broadcast_to(delay[p : p + 1, :], (2 * along, 2 * bins))
        turned = pltpu.roll(line, 0, 1, stride=1, stride_axis=0)
        table[p] = turned[:, bins:].astype(F32)
    for p in range(pings):
        pick_t[pl.ds(p * along, along), :] = table[p, pl.ds(off[p], along), :]
    picked = pick_t[...].T
    valid = ap[...].astype(F32)
    left = lanes((bins, bins)) < along
    masks = [
        jnp.where(left, valid[:, 2 * q : 2 * q + 1], valid[:, 2 * q + 1 : 2 * q + 2])
        for q in range(pings // 2)
    ]
    picked = jnp.where(jnp.concatenate(masks, axis=1) != 0.0, picked, -1.0)
    blocks = picked.shape[0] // 8
    delays_iota = lax.broadcasted_iota(jnp.int32, (blocks, DMAX, 8, depth), 1).astype(F32)
    chosen = jnp.where(picked.reshape(blocks, 1, 8, depth) == delays_iota, 1.0, 0.0)
    weight[...] = chosen.reshape(blocks * DMAX * 8, depth).astype(BF16)

    for c in range(2):
        halo_copies[c].wait_send()
    for h in range(2):
        pltpu.make_async_remote_copy(
            src_ref=head.at[h],
            dst_ref=halo.at[h],
            send_sem=halo_send.at[h],
            recv_sem=halo_recv.at[h],
            device_id={"range": below},
            device_id_type=MESH,
        ).wait_recv()
    inside = jnp.where(rng < groups - 1, 1.0, 0.0).astype(F32)
    which = (jnp.int32(0), jnp.int32(1))
    for slot, h in ((0, elev), (1, other)):
        values = halo[h].astype(F32) * inside
        for p in range(pings):
            moved = pltpu.roll(values, 128 - 32 * p, 1) if p else values
            halo_rows[slot, pl.ds(p * along, along), :] = moved.astype(BF16)
    for copy in sib_copies:
        copy.wait()

    rhs = jnp.concatenate(
        [
            jnp.concatenate([own[...].reshape(depth, half * bins), halo_rows[0]], axis=1),
            jnp.concatenate([sib[...].reshape(depth, half * bins), halo_rows[1]], axis=1),
        ],
        axis=0,
    )

    def shifted(values, count):
        lane = lanes(values.shape)
        return jnp.where(lane < bins - count, pltpu.roll(values, bins - count, 1), 0.0)

    share_copies = []
    for start in range(0, len(ROUTES), 2):
        pair = ROUTES[start : start + 2]
        targets = [target_of(ping, route) for route in pair]
        picks = jnp.concatenate(
            [weight[pl.ds(pl.multiple_of(t * 128, 128), 128), :] for t in targets], axis=0
        )
        prod = jnp.dot(
            jnp.concatenate([picks, picks], axis=1), rhs, preferred_element_type=F32
        ).reshape(4, DMAX, 8, (half + 1) * bins)

        def at(d, b):
            return prod[:, d, :, b * bins : (b + 1) * bins].reshape(32, bins)

        edge = jnp.zeros((32, bins), F32)
        lane = lanes((32, bins))
        for d in range(1, DMAX):
            edge = edge + jnp.where(
                lane % 8 >= 8 - d, pltpu.roll(at(d, half), 8 - d, 1), 0.0
            )
        images = []
        for b in range(half):
            level = [at(d, b) for d in range(DMAX)]
            step = 1
            while len(level) > 1:
                level = [
                    level[i] + shifted(level[i + 1], step) for i in range(0, len(level), 2)
                ]
                step *= 2
            end = jnp.where(lane >= bins - 8, pltpu.roll(edge, bins - 8 - 8 * b, 1), 0.0)
            images.append(level[0] + end)
        for k in range(4):
            route, side = pair[k // 2], k % 2
            slot = start + k // 2
            for b in range(0, half, 2):
                rows = jnp.concatenate(
                    [images[b][8 * k : 8 * k + 8], images[b + 1][8 * k : 8 * k + 8]], axis=0
                ).astype(BF16)
                stage[slot, side, pl.ds(8 * b, 16), :] = rows
        for i, route in enumerate(pair):
            slot = start + i
            for side in (other, elev):
                if route == (0, 0) and side is elev:
                    continue
                copy = pltpu.make_async_remote_copy(
                    src_ref=stage.at[slot, side],
                    dst_ref=got.at[slot, elev],
                    send_sem=share_send.at[slot, side],
                    recv_sem=share_recv.at[slot, elev],
                    device_id={"ping": targets[i], "elev": side},
                    device_id_type=MESH,
                )
                copy.start()
                share_copies.append(copy)

    mine = len(ROUTES) - 1
    got[mine, elev] = stage[mine, elev]
    for slot in range(len(ROUTES)):
        for h in (other, elev):
            if slot == mine and h is elev:
                continue
            pltpu.make_async_remote_copy(
                src_ref=stage.at[slot, h],
                dst_ref=got.at[slot, h],
                send_sem=share_send.at[slot, h],
                recv_sem=share_recv.at[slot, h],
                device_id={"elev": other},
                device_id_type=MESH,
            ).wait_recv()
    total = got[0].astype(F32)
    for slot in range(1, len(ROUTES)):
        total = total + got[slot].astype(F32)
    out_ref[...] = (total * scale).reshape(out_ref.shape)
    for copy in share_copies:
        copy.wait_send()


def solution(mesh):
    groups = mesh.shape["range"]
    ranks = mesh.shape["ping"]

    def body(echoes, steer, offsets, delays, aperture):
        pings, elems, along, bins = echoes.shape
        beams_count = steer.shape[1]
        half = beams_count // 2
        columns = aperture.shape[0]
        depth = pings * along
        scale = float(ranks * pings * along) ** (-0.5)
        out = pl.pallas_call(
            functools.partial(kernel, scale, groups),
            out_shape=jax.ShapeDtypeStruct((beams_count, 8, bins), F32),
            in_specs=[pl.BlockSpec(memory_space=pl.ANY)] * 5,
            out_specs=pl.BlockSpec(memory_space=pltpu.VMEM),
            scratch_shapes=[
                pltpu.VMEM(echoes.shape, BF16),
                pltpu.VMEM(steer.shape, BF16),
                pltpu.SMEM(offsets.shape, jnp.int32),
                pltpu.VMEM(delays.shape, jnp.int32),
                pltpu.VMEM(aperture.shape, jnp.int32),
                pltpu.VMEM((beams_count, elems, 8, bins), F32),
                pltpu.VMEM((elems * bins, 2 * bins), BF16),
                pltpu.VMEM((pings, 2 * along, bins), F32),
                pltpu.VMEM((columns * DMAX, depth), BF16),
                pltpu.VMEM((depth, columns), F32),
                pltpu.VMEM((2, along, bins), BF16),
                pltpu.VMEM((2, along, bins), BF16),
                pltpu.VMEM((pings, along, half * bins), BF16),
                pltpu.VMEM((pings, along, half * bins), BF16),
                pltpu.VMEM((pings, along, half * bins), BF16),
                pltpu.VMEM((2, depth, bins), BF16),
                pltpu.VMEM((len(ROUTES), 2, half * 8, bins), BF16),
                pltpu.VMEM((len(ROUTES), 2, half * 8, bins), BF16),
                pltpu.SemaphoreType.DMA((pings,)),
                pltpu.SemaphoreType.DMA((4,)),
                pltpu.SemaphoreType.DMA((2,)),
                pltpu.SemaphoreType.DMA((2,)),
                pltpu.SemaphoreType.DMA((pings,)),
                pltpu.SemaphoreType.DMA((pings,)),
                pltpu.SemaphoreType.DMA((len(ROUTES), 2)),
                pltpu.SemaphoreType.DMA((len(ROUTES), 2)),
            ],
            compiler_params=pltpu.CompilerParams(
                collective_id=0, has_side_effects=True, vmem_limit_bytes=40 * 2**20
            ),
            cost_estimate=pl.CostEstimate(
                flops=2 * columns * DMAX * depth * beams_count * bins,
                bytes_accessed=echoes.size * 2,
                transcendentals=0,
            ),
        )(echoes, steer, offsets, delays, aperture)
        return jnp.transpose(out, (1, 0, 2)).astype(BF16)

    placed = (
        P("ping", "elev", None, "range"),
        P("elev", None, "range"),
        P("ping"),
        P("ping", None),
        P(None, "ping"),
    )
    return jax.shard_map(
        body,
        mesh=mesh,
        in_specs=placed,
        out_specs=P(("ping", "elev"), None, "range"),
        check_vma=False,
    )
```

```python
import functools

import jax
import jax.numpy as jnp
from jax import lax
from jax.experimental import pallas as pl
from jax.experimental.pallas import tpu as pltpu
from jax.sharding import PartitionSpec as P

MESH = pl.DeviceIdType.MESH
DMAX = 8
F32 = jnp.float32
BF16 = jnp.bfloat16

ROUTES = ((2, 1), (2, 0), (1, 1), (3, 1), (0, 1), (1, 0), (3, 0), (0, 0))


def target_of(ping, route):
    steps, flip = route
    y, far = ping // 2, ping % 2
    return ((y + steps) % 4) * 2 + (far + flip) % 2


def lanes(shape):
    return lax.broadcasted_iota(jnp.int32, shape, len(shape) - 1)


def kernel(
    scale, groups,
    echo_hbm, steer_hbm, off_hbm, delay_hbm, ap_hbm, out_ref,
    echo, steer, off, delay, ap, spread, table, pick_t, weight, rhs,
    stage, stage_edge, got, got_edge,
    in_sem, small_sem, share_send, share_recv, edge_send, edge_recv,
):
    ping = lax.axis_index("ping")
    rng = lax.axis_index("range")
    elev = lax.axis_index("elev")
    other = 1 - elev
    sides = (other, elev)
    pings, elems, along, bins = echo.shape
    beams = steer.shape[1]
    depth = pings * along

    loads = [
        pltpu.make_async_copy(src, dst, small_sem.at[i])
        for i, (src, dst) in enumerate(
            ((steer_hbm, steer), (delay_hbm, delay), (off_hbm, off), (ap_hbm, ap))
        )
    ]
    for load in loads:
        load.start()
    echo_loads = [
        pltpu.make_async_copy(echo_hbm.at[p], echo.at[p], in_sem.at[p]) for p in range(pings)
    ]
    for load in echo_loads:
        load.start()

    barrier = pltpu.get_barrier_semaphore()
    for route in ROUTES:
        for side in sides:
            if route != (0, 0) or side is other:
                pl.semaphore_signal(
                    barrier, inc=1, device_id_type=MESH,
                    device_id={"ping": target_of(ping, route), "elev": side},
                )

    @pl.when(rng < groups - 1)
    def _():
        for route in ROUTES:
            for side in sides:
                pl.semaphore_signal(
                    barrier, inc=1, device_id_type=MESH,
                    device_id={"ping": target_of(ping, route), "range": rng + 1, "elev": side},
                )

    for load in loads:
        load.wait()
    for p in range(pings):
        line = jnp.broadcast_to(delay[p : p + 1, :], (2 * along, 2 * bins))
        turned = pltpu.roll(line, 0, 1, stride=1, stride_axis=0)
        table[p] = turned[:, bins:].astype(F32)
    for p in range(pings):
        valid = ap[p : p + 1, :] != 0
        picked = table[p, pl.ds(off[p], along), :]
        pick_t[pl.ds(p * along, along), :] = jnp.where(valid, picked, -1.0)
    picked = pick_t[...].T
    blocks = picked.shape[0] // 8
    delays_iota = lax.broadcasted_iota(jnp.int32, (blocks, DMAX, 8, depth), 1).astype(F32)
    chosen = jnp.where(picked.reshape(blocks, 1, 8, depth) == delays_iota, 1.0, 0.0)
    weight[...] = chosen.reshape(blocks * DMAX * 8, depth).astype(BF16)

    for e in range(elems):
        rows = steer[e].astype(F32)
        for b in range(beams):
            spread[b, e] = jnp.broadcast_to(rows[b : b + 1], (8, bins))
    for load in echo_loads:
        load.wait()
    for p in range(pings):

        def tile(i, carry, p=p):
            start = pl.multiple_of(i * 16, 16)
            rows = pl.ds(pl.multiple_of(p * along + i * 16, 16), 16)
            values = [echo[p, e, pl.ds(start, 16), :].astype(F32) for e in range(elems)]
            lane = lanes((16, bins))
            heads = jnp.zeros((16, bins), F32)
            for b in range(beams):
                total = None
                for e in range(elems):
                    line = spread[b, e]
                    term = values[e] * jnp.concatenate([line, line], axis=0)
                    total = term if total is None else total + term
                rhs[rows, pl.ds(b * bins, bins)] = total.astype(BF16)
                first = jnp.where(lane < 8, total, 0.0)
                heads = heads + (pltpu.roll(first, 8 * b, 1) if b else first)
            rhs[rows, pl.ds(beams * bins, bins)] = heads.astype(BF16)
            return carry

        lax.fori_loop(0, along // 16, tile, 0)

    pl.semaphore_wait(barrier, 2 * len(ROUTES) - 1 + jnp.where(rng > 0, 2 * len(ROUTES), 0))

    def shifted(values, count):
        lane = lanes(values.shape)
        return jnp.where(lane < bins - count, pltpu.roll(values, bins - count, 1), 0.0)

    share_copies = []
    edge_copies = []
    for start in range(0, len(ROUTES), 2):
        pair = ROUTES[start : start + 2]
        targets = [target_of(ping, route) for route in pair]
        picks = jnp.concatenate(
            [weight[pl.ds(pl.multiple_of(t * 128, 128), 128), :] for t in targets], axis=0
        )

        def product(low, high):
            block = jnp.dot(
                picks, rhs[:, pl.ds(low * bins, (high - low) * bins)], preferred_element_type=F32
            )
            return block.reshape(4, DMAX, 8, (high - low) * bins)

        for b in range(0, beams, 2):
            prod = product(b, b + 2)
            images = []
            for c in range(2):
                level = [
                    prod[:, d, :, c * bins : (c + 1) * bins].reshape(32, bins) for d in range(DMAX)
                ]
                step = 1
                while len(level) > 1:
                    level = [
                        level[i] + shifted(level[i + 1], step) for i in range(0, len(level), 2)
                    ]
                    step *= 2
                images.append(level[0])
            for k in range(4):
                rows = jnp.concatenate([image[8 * k : 8 * k + 8] for image in images], axis=0)
                stage[start + k // 2, k % 2, pl.ds(8 * b, 16), :] = rows.astype(BF16)
        prod = product(beams, beams + 1)
        lane = lanes((32, bins))
        edge = jnp.zeros((32, bins), F32)
        for d in range(1, DMAX):
            part = pltpu.roll(prod[:, d].reshape(32, bins), 8 - d, 1)
            edge = edge + jnp.where(lane % 8 >= 8 - d, part, 0.0)
        for i in range(2):
            stage_edge[start + i] = edge[16 * i : 16 * i + 16].astype(BF16)

        for i, route in enumerate(pair):
            slot = start + i
            for side in sides:
                if route == (0, 0) and side is elev:
                    continue
                copy = pltpu.make_async_remote_copy(
                    src_ref=stage.at[slot, side],
                    dst_ref=got.at[slot, elev],
                    send_sem=share_send.at[slot, side],
                    recv_sem=share_recv.at[slot, elev],
                    device_id={"ping": targets[i], "elev": side},
                    device_id_type=MESH,
                )
                copy.start()
                share_copies.append(copy)

        @pl.when(rng > 0)
        def _(start=start, targets=targets):
            for i in range(2):
                slot = start + i
                for side in sides:
                    copy = pltpu.make_async_remote_copy(
                        src_ref=stage_edge.at[slot],
                        dst_ref=got_edge.at[slot, elev],
                        send_sem=edge_send.at[slot, side],
                        recv_sem=edge_recv.at[slot, elev],
                        device_id={"ping": targets[i], "range": rng - 1, "elev": side},
                        device_id_type=MESH,
                    )
                    copy.start()

    def share_of(slot, h):
        return pltpu.make_async_remote_copy(
            src_ref=stage.at[slot, h],
            dst_ref=got.at[slot, h],
            send_sem=share_send.at[slot, h],
            recv_sem=share_recv.at[slot, h],
            device_id={"elev": other},
            device_id_type=MESH,
        )

    def edge_of(slot, h):
        return pltpu.make_async_remote_copy(
            src_ref=stage_edge.at[slot],
            dst_ref=got_edge.at[slot, h],
            send_sem=edge_send.at[slot, h],
            recv_sem=edge_recv.at[slot, h],
            device_id={"elev": other},
            device_id_type=MESH,
        )

    mine = len(ROUTES) - 1
    total = stage[mine, elev].astype(F32)
    for slot in range(len(ROUTES)):
        for h in sides:
            if slot == mine and h is elev:
                continue
            share_of(slot, h).wait_recv()
            total = total + got[slot, h].astype(F32)

    @pl.when(rng < groups - 1)
    def _():
        for slot in range(len(ROUTES)):
            for h in sides:
                edge_of(slot, h).wait_recv()

    @pl.when(rng == groups - 1)
    def _():
        got_edge[...] = jnp.zeros_like(got_edge)

    edge = jnp.zeros((16, bins), F32)
    for slot in range(len(ROUTES)):
        for h in range(2):
            edge = edge + got_edge[slot, h].astype(F32)
    edge = jnp.where(elev == 0, edge[:8], edge[8:])
    lane = lanes((8, bins))
    for b in range(beams):
        end = jnp.where(lane >= bins - 8, pltpu.roll(edge, bins - 8 - 8 * b, 1), 0.0)
        out_ref[b] = (total[8 * b : 8 * b + 8] + end) * scale

    for copy in share_copies:
        copy.wait_send()

    @pl.when(rng > 0)
    def _():
        for slot in range(len(ROUTES)):
            for h in sides:
                edge_of(slot, h).wait_send()


def solution(mesh):
    groups = mesh.shape["range"]
    ranks = mesh.shape["ping"]

    def body(echoes, steer, offsets, delays, aperture):
        pings, elems, along, bins = echoes.shape
        beams = steer.shape[1]
        columns = aperture.shape[0]
        depth = pings * along
        scale = float(ranks * pings * along) ** (-0.5)
        slots = (len(ROUTES), 2)
        out = pl.pallas_call(
            functools.partial(kernel, scale, groups),
            out_shape=jax.ShapeDtypeStruct((beams, 8, bins), F32),
            in_specs=[pl.BlockSpec(memory_space=pltpu.HBM)] * 5,
            out_specs=pl.BlockSpec(memory_space=pltpu.VMEM),
            scratch_shapes=[
                pltpu.VMEM(echoes.shape, BF16),
                pltpu.VMEM(steer.shape, BF16),
                pltpu.SMEM(offsets.shape, jnp.int32),
                pltpu.VMEM(delays.shape, jnp.int32),
                pltpu.VMEM((pings, columns), jnp.int32),
                pltpu.VMEM((beams, elems, 8, bins), F32),
                pltpu.VMEM((pings, 2 * along, bins), F32),
                pltpu.VMEM((depth, columns), F32),
                pltpu.VMEM((columns * DMAX, depth), BF16),
                pltpu.VMEM((depth, (beams + 1) * bins), BF16),
                pltpu.VMEM(slots + (beams * 8, bins), BF16),
                pltpu.VMEM((len(ROUTES), 16, bins), BF16),
                pltpu.VMEM(slots + (beams * 8, bins), BF16),
                pltpu.VMEM(slots + (16, bins), BF16),
                pltpu.SemaphoreType.DMA((pings,)),
                pltpu.SemaphoreType.DMA((4,)),
                pltpu.SemaphoreType.DMA(slots),
                pltpu.SemaphoreType.DMA(slots),
                pltpu.SemaphoreType.DMA(slots),
                pltpu.SemaphoreType.DMA(slots),
            ],
            compiler_params=pltpu.CompilerParams(
                collective_id=0, has_side_effects=True, vmem_limit_bytes=60 * 2**20
            ),
            cost_estimate=pl.CostEstimate(
                flops=2 * columns * DMAX * depth * beams * bins,
                bytes_accessed=echoes.size * 2,
                transcendentals=0,
            ),
        )(echoes, steer, offsets, delays, jnp.transpose(aperture))
        return jnp.transpose(out, (1, 0, 2)).astype(BF16)

    placed = (
        P("ping", "elev", None, "range"),
        P("elev", None, "range"),
        P("ping"),
        P("ping", None),
        P(None, "ping"),
    )
    return jax.shard_map(
        body,
        mesh=mesh,
        in_specs=placed,
        out_specs=P(("ping", "elev"), None, "range"),
        check_vma=False,
    )
```

```python
import functools

import jax
import jax.numpy as jnp
from jax import lax
from jax.experimental import pallas as pl
from jax.experimental.pallas import tpu as pltpu
from jax.sharding import PartitionSpec as P

MESH = pl.DeviceIdType.MESH
DMAX = 8
F32 = jnp.float32
BF16 = jnp.bfloat16

ROUTES = ((2, 1), (2, 0), (1, 1), (3, 1), (0, 1), (1, 0), (3, 0), (0, 0))


def target_of(ping, route):
    steps, flip = route
    y, far = ping // 2, ping % 2
    return ((y + steps) % 4) * 2 + (far + flip) % 2


def lanes(shape):
    return lax.broadcasted_iota(jnp.int32, shape, len(shape) - 1)


def kernel(
    scale, groups,
    echo_hbm, steer_hbm, off_hbm, delay_hbm, ap_hbm, out_ref,
    echo, steer, off, delay, ap, spread, table, pick_t, weight, rhs, result,
    stage, stage_edge, got, got_edge,
    in_sem, small_sem, share_send, share_recv, edge_send, edge_recv,
):
    ping = lax.axis_index("ping")
    rng = lax.axis_index("range")
    elev = lax.axis_index("elev")
    other = 1 - elev
    sides = (other, elev)
    pings, elems, along, bins = echo.shape
    beams = steer.shape[1]
    depth = pings * along

    loads = [
        pltpu.make_async_copy(src, dst, small_sem.at[i])
        for i, (src, dst) in enumerate(
            ((steer_hbm, steer), (delay_hbm, delay), (off_hbm, off), (ap_hbm, ap))
        )
    ]
    for load in loads:
        load.start()
    echo_loads = [
        pltpu.make_async_copy(echo_hbm.at[p], echo.at[p], in_sem.at[p]) for p in range(pings)
    ]
    for load in echo_loads:
        load.start()

    barrier = pltpu.get_barrier_semaphore()
    for route in ROUTES:
        for side in sides:
            if route != (0, 0) or side is other:
                pl.semaphore_signal(
                    barrier, inc=1, device_id_type=MESH,
                    device_id={"ping": target_of(ping, route), "elev": side},
                )

    @pl.when(rng < groups - 1)
    def _():
        for route in ROUTES:
            for side in sides:
                pl.semaphore_signal(
                    barrier, inc=1, device_id_type=MESH,
                    device_id={"ping": target_of(ping, route), "range": rng + 1, "elev": side},
                )

    for load in loads:
        load.wait()
    for p in range(pings):
        line = jnp.broadcast_to(delay[p : p + 1, :], (2 * along, 2 * bins))
        turned = pltpu.roll(line, 0, 1, stride=1, stride_axis=0)
        table[p] = turned[:, bins:].astype(F32)
    for p in range(pings):
        valid = ap[p : p + 1, :] != 0
        picked = table[p, pl.ds(off[p], along), :]
        pick_t[pl.ds(p * along, along), :] = jnp.where(valid, picked, -1.0)
    picked = pick_t[...].T.astype(BF16)
    columns = picked.shape[0]
    one, zero = jnp.ones((), BF16), jnp.zeros((), BF16)
    for high in range(2):
        for low in range(4):
            weight[pl.ds(high * columns, columns), pl.ds(low * depth, depth)] = jnp.where(
                picked == 4 * high + low, one, zero
            )

    for e in range(elems):
        rows = steer[e].astype(F32)
        for b in range(beams):
            spread[b, e] = jnp.broadcast_to(rows[b : b + 1], (8, bins))
    for load in echo_loads:
        load.wait()

    def later(values, count):
        moved = pltpu.roll(values, bins - count, 1)
        return jnp.where(lanes(values.shape) < bins - count, moved, jnp.zeros((), values.dtype))

    lane = lanes((depth, bins))
    heads = jnp.zeros((depth, bins), BF16)
    for b in range(beams):
        rows = []
        for p in range(pings):
            total = None
            for e in range(elems):
                line = jnp.concatenate([spread[b, e]] * (along // 8), axis=0)
                term = echo[p, e].astype(F32) * line
                total = term if total is None else total + term
            rows.append(total.astype(BF16))
        beam = jnp.concatenate(rows, axis=0)
        place = pl.ds(b % 2 * bins, bins)
        rhs[b // 2, pl.ds(0, depth), place] = beam
        for low in range(1, 4):
            rhs[b // 2, pl.ds(low * depth, depth), place] = later(beam, low)
        here = (lane >= 16 * b + 8) & (lane < 16 * b + 16)
        heads = jnp.where(here, pltpu.roll(beam, 16 * b + 8, 1), heads)
        if b % 2:
            prod = jnp.dot(weight[...], rhs[b // 2], preferred_element_type=F32)
            images = [
                prod[:columns, c * bins : (c + 1) * bins]
                + later(prod[columns:, c * bins : (c + 1) * bins], 4)
                for c in range(2)
            ]
            for j in range(columns // 8):
                rows = jnp.concatenate([image[8 * j : 8 * j + 8] for image in images], axis=0)
                stage[j // 2, j % 2, pl.ds(8 * (b - 1), 16), :] = rows.astype(BF16)
    heads = [heads] + [pltpu.roll(heads, bins - low, 1) for low in range(1, 4)]
    prod = jnp.dot(weight[...], jnp.concatenate(heads, axis=0), preferred_element_type=F32)
    edge = prod[:columns] + pltpu.roll(prod[columns:], bins - 4, 1)
    for t in range(columns // 16):
        stage_edge[t] = edge[16 * t : 16 * t + 16].astype(BF16)

    pl.semaphore_wait(barrier, 2 * len(ROUTES) - 1 + jnp.where(rng > 0, 2 * len(ROUTES), 0))
    share_copies = []
    for slot, route in enumerate(ROUTES):
        target = target_of(ping, route)
        for side in sides:
            if route == (0, 0) and side is elev:
                continue
            copy = pltpu.make_async_remote_copy(
                src_ref=stage.at[target, side],
                dst_ref=got.at[slot, elev],
                send_sem=share_send.at[slot, side],
                recv_sem=share_recv.at[slot, elev],
                device_id={"ping": target, "elev": side},
                device_id_type=MESH,
            )
            copy.start()
            share_copies.append(copy)

    @pl.when(rng > 0)
    def _():
        for slot, route in enumerate(ROUTES):
            target = target_of(ping, route)
            for side in sides:
                copy = pltpu.make_async_remote_copy(
                    src_ref=stage_edge.at[target],
                    dst_ref=got_edge.at[slot, elev],
                    send_sem=edge_send.at[slot, side],
                    recv_sem=edge_recv.at[slot, elev],
                    device_id={"ping": target, "range": rng - 1, "elev": side},
                    device_id_type=MESH,
                )
                copy.start()

    def share_of(slot, h):
        return pltpu.make_async_remote_copy(
            src_ref=stage.at[slot, h],
            dst_ref=got.at[slot, h],
            send_sem=share_send.at[slot, h],
            recv_sem=share_recv.at[slot, h],
            device_id={"elev": other},
            device_id_type=MESH,
        )

    def edge_of(slot, h):
        return pltpu.make_async_remote_copy(
            src_ref=stage_edge.at[slot],
            dst_ref=got_edge.at[slot, h],
            send_sem=edge_send.at[slot, h],
            recv_sem=edge_recv.at[slot, h],
            device_id={"elev": other},
            device_id_type=MESH,
        )

    mine = len(ROUTES) - 1
    total = stage[ping, elev].astype(F32)
    for slot in range(len(ROUTES)):
        for h in sides:
            if slot == mine and h is elev:
                continue
            share_of(slot, h).wait_recv()
            total = total + got[slot, h].astype(F32)

    @pl.when(rng < groups - 1)
    def _():
        for slot in range(len(ROUTES)):
            for h in sides:
                edge_of(slot, h).wait_recv()

    @pl.when(rng == groups - 1)
    def _():
        got_edge[...] = jnp.zeros_like(got_edge)

    edge = jnp.zeros((16, bins), F32)
    for slot in range(len(ROUTES)):
        for h in range(2):
            edge = edge + got_edge[slot, h].astype(F32)
    edge = jnp.where(elev == 0, edge[:8], edge[8:])
    lane = lanes((8, bins))
    for b in range(beams):
        moved = pltpu.roll(edge, (2 * bins - 8 - 16 * b) % bins, 1)
        end = jnp.where(lane >= bins - 8, moved, 0.0)
        result[:, b, :] = (total[8 * b : 8 * b + 8] + end) * scale
    out_ref[...] = result[...].astype(BF16)

    for copy in share_copies:
        copy.wait_send()

    @pl.when(rng > 0)
    def _():
        for slot in range(len(ROUTES)):
            for h in sides:
                edge_of(slot, h).wait_send()


def solution(mesh):
    groups = mesh.shape["range"]
    ranks = mesh.shape["ping"]

    def body(echoes, steer, offsets, delays, aperture):
        pings, elems, along, bins = echoes.shape
        beams = steer.shape[1]
        columns = aperture.shape[0]
        depth = pings * along
        scale = float(ranks * pings * along) ** (-0.5)
        slots = (len(ROUTES), 2)
        return pl.pallas_call(
            functools.partial(kernel, scale, groups),
            out_shape=jax.ShapeDtypeStruct((8, beams, bins), BF16),
            in_specs=[pl.BlockSpec(memory_space=pltpu.HBM)] * 5,
            out_specs=pl.BlockSpec(memory_space=pltpu.VMEM),
            scratch_shapes=[
                pltpu.VMEM(echoes.shape, BF16),
                pltpu.VMEM(steer.shape, BF16),
                pltpu.SMEM(offsets.shape, jnp.int32),
                pltpu.VMEM(delays.shape, jnp.int32),
                pltpu.VMEM((pings, columns), jnp.int32),
                pltpu.VMEM((beams, elems, 8, bins), F32),
                pltpu.VMEM((pings, 2 * along, bins), F32),
                pltpu.VMEM((depth, columns), F32),
                pltpu.VMEM((2 * columns, 4 * depth), BF16),
                pltpu.VMEM((beams // 2, 4 * depth, 2 * bins), BF16),
                pltpu.VMEM((8, beams, bins), F32),
                pltpu.VMEM(slots + (beams * 8, bins), BF16),
                pltpu.VMEM((len(ROUTES), 16, bins), BF16),
                pltpu.VMEM(slots + (beams * 8, bins), BF16),
                pltpu.VMEM(slots + (16, bins), BF16),
                pltpu.SemaphoreType.DMA((pings,)),
                pltpu.SemaphoreType.DMA((4,)),
                pltpu.SemaphoreType.DMA(slots),
                pltpu.SemaphoreType.DMA(slots),
                pltpu.SemaphoreType.DMA(slots),
                pltpu.SemaphoreType.DMA(slots),
            ],
            compiler_params=pltpu.CompilerParams(
                collective_id=0, has_side_effects=True, vmem_limit_bytes=60 * 2**20
            ),
            cost_estimate=pl.CostEstimate(
                flops=2 * columns * DMAX * depth * beams * bins,
                bytes_accessed=echoes.size * 2,
                transcendentals=0,
            ),
        )(echoes, steer, offsets, delays, jnp.transpose(aperture))

    placed = (
        P("ping", "elev", None, "range"),
        P("elev", None, "range"),
        P("ping"),
        P("ping", None),
        P(None, "ping"),
    )
    return jax.shard_map(
        body,
        mesh=mesh,
        in_specs=placed,
        out_specs=P(("ping", "elev"), None, "range"),
        check_vma=False,
    )
```

```python
import functools

import jax
import jax.numpy as jnp
from jax import lax
from jax.experimental import pallas as pl
from jax.experimental.pallas import tpu as pltpu
from jax.sharding import PartitionSpec as P

MESH = pl.DeviceIdType.MESH
DMAX = 8
AHEAD = 0
F32 = jnp.float32
BF16 = jnp.bfloat16

ROUTES = ((2, 1), (2, 0), (1, 1), (3, 1), (0, 1), (1, 0), (3, 0), (0, 0))


def target_of(ping, route):
    steps, flip = route
    y, far = ping // 2, ping % 2
    return ((y + steps) % 4) * 2 + (far + flip) % 2


def lanes(shape):
    return lax.broadcasted_iota(jnp.int32, shape, len(shape) - 1)


def kernel(
    scale, groups,
    echo_hbm, steer_hbm, off_hbm, delay_hbm, ap_hbm, out_ref,
    echo, steer, off, delay, ap, spread, table, pick_t, weight, wide, rhs, result,
    stage, stage_edge, got, got_edge,
    in_sem, small_sem, share_send, share_recv, edge_send, edge_recv,
):
    ping = lax.axis_index("ping")
    rng = lax.axis_index("range")
    elev = lax.axis_index("elev")
    other = 1 - elev
    sides = (other, elev)
    pings, elems, along, bins = echo.shape
    beams = steer.shape[1]
    depth = pings * along

    loads = [
        pltpu.make_async_copy(src, dst, small_sem.at[i])
        for i, (src, dst) in enumerate(
            ((steer_hbm, steer), (delay_hbm, delay), (off_hbm, off), (ap_hbm, ap))
        )
    ]
    for load in loads:
        load.start()
    echo_loads = [
        pltpu.make_async_copy(echo_hbm.at[p], echo.at[p], in_sem.at[p]) for p in range(pings)
    ]
    for load in echo_loads:
        load.start()

    barrier = pltpu.get_barrier_semaphore()
    for route in ROUTES:
        for side in sides:
            if route != (0, 0) or side is other:
                pl.semaphore_signal(
                    barrier, inc=1, device_id_type=MESH,
                    device_id={"ping": target_of(ping, route), "elev": side},
                )

    @pl.when(rng < groups - 1)
    def _():
        for route in ROUTES:
            for side in sides:
                pl.semaphore_signal(
                    barrier, inc=1, device_id_type=MESH,
                    device_id={"ping": target_of(ping, route), "range": rng + 1, "elev": side},
                )

    for load in loads:
        load.wait()
    for p in range(pings):
        line = jnp.broadcast_to(delay[p : p + 1, :], (2 * along, 2 * bins))
        turned = pltpu.roll(line, 0, 1, stride=1, stride_axis=0)
        table[p] = turned[:, bins:].astype(F32)
    for p in range(pings):
        valid = ap[p : p + 1, :] != 0
        picked = table[p, pl.ds(off[p], along), :]
        pick_t[pl.ds(p * along, along), :] = jnp.where(valid, picked, -1.0)
    picked = pick_t[...].T.astype(BF16)
    columns = picked.shape[0]
    one, zero = jnp.ones((), BF16), jnp.zeros((), BF16)
    for high in range(2):
        for low in range(4):
            weight[pl.ds(high * columns, columns), pl.ds(low * depth, depth)] = jnp.where(
                picked == 4 * high + low, one, zero
            )

    wide[...] = jnp.zeros_like(wide)
    lane = lanes((beams, bins))
    row = lax.broadcasted_iota(jnp.int32, (beams, bins), 0)
    for e in range(elems):
        rows = steer[e].astype(F32)
        for b in range(beams):
            spread[b, e] = jnp.broadcast_to(rows[b : b + 1], (8, bins))
        moved = pltpu.roll(jnp.where(lane < 8, rows, 0.0), 8, 1, stride=16, stride_axis=0)
        line = jnp.sum(moved, axis=0, keepdims=True)
        diag = jnp.where(lane % 16 - 8 == row, line, 0.0)
        diag = jnp.concatenate([diag, jnp.zeros_like(diag)], axis=0)
        wide[pl.ds(e * bins, 16), :] = diag.astype(BF16)

    def later(values, count):
        moved = pltpu.roll(values, bins - count, 1)
        return jnp.where(lanes(values.shape) < bins - count, moved, jnp.zeros((), values.dtype))

    for load in echo_loads:
        load.wait()

    flat = [jnp.concatenate([echo[p, e] for e in range(elems)], axis=1) for p in range(pings)]
    heads = jnp.dot(jnp.concatenate(flat, axis=0), wide[...], preferred_element_type=F32)
    heads = heads.astype(BF16)
    heads = [heads] + [pltpu.roll(heads, bins - low, 1) for low in range(1, 4)]
    prod = jnp.dot(weight[...], jnp.concatenate(heads, axis=0), preferred_element_type=F32)
    edge = prod[:columns] + pltpu.roll(prod[columns:], bins - 4, 1)
    for t in range(columns // 16):
        stage_edge[t] = edge[16 * t : 16 * t + 16].astype(BF16)

    def make_beam(b):
        rows = []
        for p in range(pings):
            total = None
            for e in range(elems):
                line = jnp.concatenate([spread[b, e]] * (along // 8), axis=0)
                term = echo[p, e].astype(F32) * line
                total = term if total is None else total + term
            rows.append(total.astype(BF16))
        beam = jnp.concatenate(rows, axis=0)
        place = pl.ds(b % 2 * bins, bins)
        rhs[b // 2, pl.ds(0, depth), place] = beam
        for low in range(1, 4):
            rhs[b // 2, pl.ds(low * depth, depth), place] = later(beam, low)

    def project(q):
        prod = jnp.dot(weight[...], rhs[q], preferred_element_type=F32)
        images = [
            prod[:columns, c * bins : (c + 1) * bins]
            + later(prod[columns:, c * bins : (c + 1) * bins], 4)
            for c in range(2)
        ]
        for j in range(columns // 8):
            rows = jnp.concatenate([image[8 * j : 8 * j + 8] for image in images], axis=0)
            stage[j // 2, j % 2, pl.ds(16 * q, 16), :] = rows.astype(BF16)

    share_copies = []

    def send(q):
        for slot, route in enumerate(ROUTES):
            target = target_of(ping, route)
            for side in sides:
                if route == (0, 0) and side is elev:
                    continue
                copy = pltpu.make_async_remote_copy(
                    src_ref=stage.at[target, side, pl.ds(16 * q, 16)],
                    dst_ref=got.at[slot, elev, pl.ds(16 * q, 16)],
                    send_sem=share_send.at[slot, side, q],
                    recv_sem=share_recv.at[slot, elev, q],
                    device_id={"ping": target, "elev": side},
                    device_id_type=MESH,
                )
                copy.start()
                share_copies.append(copy)

    for b in range(2 * AHEAD + 2):
        make_beam(b)
    for q in range(AHEAD):
        project(q)
    for q in range(AHEAD, beams // 2):
        if q > AHEAD:
            for b in (2 * q, 2 * q + 1):
                make_beam(b)
        project(q)
        if q == AHEAD:
            pl.semaphore_wait(
                barrier, 2 * len(ROUTES) - 1 + jnp.where(rng > 0, 2 * len(ROUTES), 0)
            )

            @pl.when(rng > 0)
            def _():
                for slot, route in enumerate(ROUTES):
                    target = target_of(ping, route)
                    for side in sides:
                        copy = pltpu.make_async_remote_copy(
                            src_ref=stage_edge.at[target],
                            dst_ref=got_edge.at[slot, elev],
                            send_sem=edge_send.at[slot, side],
                            recv_sem=edge_recv.at[slot, elev],
                            device_id={"ping": target, "range": rng - 1, "elev": side},
                            device_id_type=MESH,
                        )
                        copy.start()

            for early in range(q):
                send(early)
        send(q)

    def share_of(slot, h, q):
        return pltpu.make_async_remote_copy(
            src_ref=stage.at[slot, h, pl.ds(16 * q, 16)],
            dst_ref=got.at[slot, h, pl.ds(16 * q, 16)],
            send_sem=share_send.at[slot, h, q],
            recv_sem=share_recv.at[slot, h, q],
            device_id={"elev": other},
            device_id_type=MESH,
        )

    def edge_of(slot, h):
        return pltpu.make_async_remote_copy(
            src_ref=stage_edge.at[slot],
            dst_ref=got_edge.at[slot, h],
            send_sem=edge_send.at[slot, h],
            recv_sem=edge_recv.at[slot, h],
            device_id={"elev": other},
            device_id_type=MESH,
        )

    @pl.when(rng < groups - 1)
    def _():
        for slot in range(len(ROUTES)):
            for h in sides:
                edge_of(slot, h).wait_recv()

    @pl.when(rng == groups - 1)
    def _():
        got_edge[...] = jnp.zeros_like(got_edge)

    edge = jnp.zeros((16, bins), F32)
    for slot in range(len(ROUTES)):
        for h in range(2):
            edge = edge + got_edge[slot, h].astype(F32)
    edge = jnp.where(elev == 0, edge[:8], edge[8:])
    mine = len(ROUTES) - 1
    for q in range(beams // 2):
        part = pl.ds(16 * q, 16)
        total = stage[ping, elev, part, :].astype(F32)
        for slot in range(len(ROUTES)):
            for h in sides:
                if slot != mine or h is other:
                    share_of(slot, h, q).wait_recv()
                    total = total + got[slot, h, part, :].astype(F32)
        for b in (2 * q, 2 * q + 1):
            moved = pltpu.roll(edge, (2 * bins - 8 - 16 * b) % bins, 1)
            end = jnp.where(lane >= bins - 8, moved, 0.0)
            result[:, b, :] = (total[8 * (b % 2) : 8 * (b % 2) + 8] + end) * scale
    out_ref[...] = result[...].astype(BF16)

    for copy in share_copies:
        copy.wait_send()

    @pl.when(rng > 0)
    def _():
        for slot in range(len(ROUTES)):
            for h in sides:
                edge_of(slot, h).wait_send()


def solution(mesh):
    groups = mesh.shape["range"]
    ranks = mesh.shape["ping"]

    def body(echoes, steer, offsets, delays, aperture):
        pings, elems, along, bins = echoes.shape
        beams = steer.shape[1]
        columns = aperture.shape[0]
        depth = pings * along
        scale = float(ranks * pings * along) ** (-0.5)
        slots = (len(ROUTES), 2)
        operands = (echoes, steer, offsets, delays, jnp.transpose(aperture))
        operands = [pltpu.with_memory_space_constraint(v, pltpu.HBM) for v in operands]
        return pl.pallas_call(
            functools.partial(kernel, scale, groups),
            out_shape=jax.ShapeDtypeStruct((8, beams, bins), BF16),
            in_specs=[pl.BlockSpec(memory_space=pltpu.HBM)] * 5,
            out_specs=pl.BlockSpec(memory_space=pltpu.VMEM),
            scratch_shapes=[
                pltpu.VMEM(echoes.shape, BF16),
                pltpu.VMEM(steer.shape, BF16),
                pltpu.SMEM(offsets.shape, jnp.int32),
                pltpu.VMEM(delays.shape, jnp.int32),
                pltpu.VMEM((pings, columns), jnp.int32),
                pltpu.VMEM((beams, elems, 8, bins), F32),
                pltpu.VMEM((pings, 2 * along, bins), F32),
                pltpu.VMEM((depth, columns), F32),
                pltpu.VMEM((2 * columns, 4 * depth), BF16),
                pltpu.VMEM((elems * bins, bins), BF16),
                pltpu.VMEM((beams // 2, 4 * depth, 2 * bins), BF16),
                pltpu.VMEM((8, beams, bins), F32),
                pltpu.VMEM(slots + (beams * 8, bins), BF16),
                pltpu.VMEM((len(ROUTES), 16, bins), BF16),
                pltpu.VMEM(slots + (beams * 8, bins), BF16),
                pltpu.VMEM(slots + (16, bins), BF16),
                pltpu.SemaphoreType.DMA((pings,)),
                pltpu.SemaphoreType.DMA((4,)),
                pltpu.SemaphoreType.DMA(slots + (beams // 2,)),
                pltpu.SemaphoreType.DMA(slots + (beams // 2,)),
                pltpu.SemaphoreType.DMA(slots),
                pltpu.SemaphoreType.DMA(slots),
            ],
            compiler_params=pltpu.CompilerParams(
                collective_id=0, has_side_effects=True, vmem_limit_bytes=40 * 2**20
            ),
            cost_estimate=pl.CostEstimate(
                flops=2 * columns * DMAX * depth * beams * bins,
                bytes_accessed=echoes.size * 2,
                transcendentals=0,
            ),
        )(*operands)

    placed = (
        P("ping", "elev", None, "range"),
        P("elev", None, "range"),
        P("ping"),
        P("ping", None),
        P(None, "ping"),
    )
    return jax.shard_map(
        body,
        mesh=mesh,
        in_specs=placed,
        out_specs=P(("ping", "elev"), None, "range"),
        check_vma=False,
    )
```

```python
import functools

import jax
import jax.numpy as jnp
from jax import lax
from jax.experimental import pallas as pl
from jax.experimental.pallas import tpu as pltpu
from jax.sharding import PartitionSpec as P

MESH = pl.DeviceIdType.MESH
DMAX = 8
PIECES = 2
F32 = jnp.float32
BF16 = jnp.bfloat16

ROUTES = ((2, 1), (2, 0), (1, 1), (3, 1), (0, 1), (1, 0), (3, 0), (0, 0))


def target_of(ping, route):
    steps, flip = route
    y, far = ping // 2, ping % 2
    return ((y + steps) % 4) * 2 + (far + flip) % 2


def lanes(shape):
    return lax.broadcasted_iota(jnp.int32, shape, len(shape) - 1)


def kernel(
    scale, groups,
    echo_hbm, steer_hbm, off_hbm, delay_hbm, ap_hbm, out_ref,
    echo, steer, off, delay, ap, spread, table, pick_t, weight, wide, rhs, result,
    stage, stage_edge, got, got_edge,
    small_sem, share_send, share_recv, edge_send, edge_recv,
):
    ping = lax.axis_index("ping")
    rng = lax.axis_index("range")
    elev = lax.axis_index("elev")
    other = 1 - elev
    sides = (other, elev)
    pings, elems, along, bins = echo.shape
    beams = steer.shape[1]
    depth = pings * along

    loads = [
        pltpu.make_async_copy(src, dst, small_sem.at[i])
        for i, (src, dst) in enumerate(
            ((steer_hbm, steer), (delay_hbm, delay), (off_hbm, off), (ap_hbm, ap))
        )
    ]
    for load in loads:
        load.start()
    echo_load = pltpu.make_async_copy(echo_hbm, echo, small_sem.at[4])
    echo_load.start()

    barrier = pltpu.get_barrier_semaphore()
    for route in ROUTES:
        for side in sides:
            if route != (0, 0) or side is other:
                pl.semaphore_signal(
                    barrier, inc=1, device_id_type=MESH,
                    device_id={"ping": target_of(ping, route), "elev": side},
                )

    @pl.when(rng < groups - 1)
    def _():
        for route in ROUTES:
            for side in sides:
                pl.semaphore_signal(
                    barrier, inc=1, device_id_type=MESH,
                    device_id={"ping": target_of(ping, route), "range": rng + 1, "elev": side},
                )

    for load in loads:
        load.wait()
    for p in range(pings):
        line = jnp.broadcast_to(delay[p : p + 1, :], (2 * along, 2 * bins))
        turned = pltpu.roll(line, 0, 1, stride=1, stride_axis=0)
        table[p] = turned[:, bins:].astype(F32)
    for p in range(pings):
        valid = ap[p : p + 1, :] != 0
        picked = table[p, pl.ds(off[p], along), :]
        pick_t[pl.ds(p * along, along), :] = jnp.where(valid, picked, -1.0)
    picked = pick_t[...].T.astype(BF16)
    columns = picked.shape[0]
    one, zero = jnp.ones((), BF16), jnp.zeros((), BF16)
    for high in range(2):
        for low in range(4):
            weight[pl.ds(high * columns, columns), pl.ds(low * depth, depth)] = jnp.where(
                picked == 4 * high + low, one, zero
            )

    wide[...] = jnp.zeros_like(wide)
    lane = lanes((beams, bins))
    row = lax.broadcasted_iota(jnp.int32, (beams, bins), 0)
    for e in range(elems):
        rows = steer[e].astype(F32)
        for b in range(beams):
            spread[b, e] = jnp.broadcast_to(rows[b : b + 1], (8, bins))
        moved = pltpu.roll(jnp.where(lane < 8, rows, 0.0), 8, 1, stride=16, stride_axis=0)
        line = jnp.sum(moved, axis=0, keepdims=True)
        diag = jnp.where(lane % 16 - 8 == row, line, 0.0)
        diag = jnp.concatenate([diag, jnp.zeros_like(diag)], axis=0)
        wide[pl.ds(e * bins, 16), :] = diag.astype(BF16)

    def later(values, count):
        moved = pltpu.roll(values, bins - count, 1)
        return jnp.where(lanes(values.shape) < bins - count, moved, jnp.zeros((), values.dtype))

    echo_load.wait()

    flat = [jnp.concatenate([echo[p, e] for e in range(elems)], axis=1) for p in range(pings)]
    heads = jnp.dot(jnp.concatenate(flat, axis=0), wide[...], preferred_element_type=F32)
    heads = heads.astype(BF16)
    heads = [heads] + [pltpu.roll(heads, bins - low, 1) for low in range(1, 4)]
    prod = jnp.dot(weight[...], jnp.concatenate(heads, axis=0), preferred_element_type=F32)
    edge = prod[:columns] + pltpu.roll(prod[columns:], bins - 4, 1)
    for t in range(columns // 16):
        stage_edge[t] = edge[16 * t : 16 * t + 16].astype(BF16)

    def make_beam(b):
        rows = []
        for p in range(pings):
            total = None
            for e in range(elems):
                line = jnp.concatenate([spread[b, e]] * (along // 8), axis=0)
                term = echo[p, e].astype(F32) * line
                total = term if total is None else total + term
            rows.append(total.astype(BF16))
        beam = jnp.concatenate(rows, axis=0)
        place = pl.ds(b % 2 * bins, bins)
        rhs[b // 2, pl.ds(0, depth), place] = beam
        for low in range(1, 4):
            rhs[b // 2, pl.ds(low * depth, depth), place] = later(beam, low)

    def project(q):
        prod = jnp.dot(weight[...], rhs[q], preferred_element_type=F32)
        images = [
            prod[:columns, c * bins : (c + 1) * bins]
            + later(prod[columns:, c * bins : (c + 1) * bins], 4)
            for c in range(2)
        ]
        for j in range(columns // 8):
            rows = jnp.concatenate([image[8 * j : 8 * j + 8] for image in images], axis=0)
            stage[j, pl.ds(16 * q, 16), :] = rows.astype(BF16)

    size = beams * 8 // PIECES

    def send(piece):
        part = pl.ds(size * piece, size)
        for slot, route in enumerate(ROUTES):
            target = target_of(ping, route)
            for side in sides:
                if route == (0, 0) and side is elev:
                    continue
                pltpu.make_async_remote_copy(
                    src_ref=stage.at[2 * target + side, part],
                    dst_ref=got.at[2 * slot + elev, part],
                    send_sem=share_send.at[piece],
                    recv_sem=share_recv.at[piece],
                    device_id={"ping": target, "elev": side},
                    device_id_type=MESH,
                ).start()

    def send_edges():
        for slot, route in enumerate(ROUTES):
            target = target_of(ping, route)
            for side in sides:
                pltpu.make_async_remote_copy(
                    src_ref=stage_edge.at[target],
                    dst_ref=got_edge.at[2 * slot + elev],
                    send_sem=edge_send,
                    recv_sem=edge_recv,
                    device_id={"ping": target, "range": rng - 1, "elev": side},
                    device_id_type=MESH,
                ).start()

    per = beams // 2 // PIECES
    for piece in range(PIECES):
        for q in range(piece * per, piece * per + per):
            make_beam(2 * q)
            make_beam(2 * q + 1)
            project(q)
        if piece == 0:
            pl.semaphore_wait(
                barrier, 2 * len(ROUTES) - 1 + jnp.where(rng > 0, 2 * len(ROUTES), 0)
            )
            pl.when(rng > 0)(send_edges)
        send(piece)

    def all_shares(piece):
        part = pl.ds(size * piece, size)
        every = pl.ds(0, 2 * len(ROUTES) - 1)
        return pltpu.make_async_remote_copy(
            src_ref=stage.at[every, part],
            dst_ref=got.at[every, part],
            send_sem=share_send.at[piece],
            recv_sem=share_recv.at[piece],
            device_id={"elev": other},
            device_id_type=MESH,
        )

    all_edges = pltpu.make_async_remote_copy(
        src_ref=got_edge,
        dst_ref=got_edge,
        send_sem=edge_send,
        recv_sem=edge_recv,
        device_id={"elev": other},
        device_id_type=MESH,
    )

    @pl.when(rng < groups - 1)
    def _():
        all_edges.wait_recv()

    @pl.when(rng == groups - 1)
    def _():
        got_edge[...] = jnp.zeros_like(got_edge)

    edge = jnp.zeros((16, bins), F32)
    for i in range(2 * len(ROUTES)):
        edge = edge + got_edge[i].astype(F32)
    edge = jnp.where(elev == 0, edge[:8], edge[8:])
    mine = len(ROUTES) - 1
    for piece in range(PIECES):
        all_shares(piece).wait_recv()
        part = pl.ds(size * piece, size)
        total = stage[2 * ping + elev, part, :].astype(F32)
        total = total + got[2 * mine + other, part, :].astype(F32)
        for i in range(2 * mine):
            total = total + got[i, part, :].astype(F32)
        for k in range(size // 8):
            b = piece * size // 8 + k
            moved = pltpu.roll(edge, (2 * bins - 8 - 16 * b) % bins, 1)
            end = jnp.where(lane >= bins - 8, moved, 0.0)
            result[:, b, :] = (total[8 * k : 8 * k + 8] + end) * scale
    out_ref[...] = result[...].astype(BF16)

    for piece in range(PIECES):
        all_shares(piece).wait_send()

    @pl.when(rng > 0)
    def _():
        all_edges.wait_send()


def solution(mesh):
    groups = mesh.shape["range"]
    ranks = mesh.shape["ping"]

    def body(echoes, steer, offsets, delays, aperture):
        pings, elems, along, bins = echoes.shape
        beams = steer.shape[1]
        columns = aperture.shape[0]
        depth = pings * along
        scale = float(ranks * pings * along) ** (-0.5)
        slots = (2 * len(ROUTES),)
        operands = (echoes, steer, offsets, delays, jnp.transpose(aperture))
        operands = [pltpu.with_memory_space_constraint(v, pltpu.HBM) for v in operands]
        return pl.pallas_call(
            functools.partial(kernel, scale, groups),
            out_shape=jax.ShapeDtypeStruct((8, beams, bins), BF16),
            in_specs=[pl.BlockSpec(memory_space=pltpu.HBM)] * 5,
            out_specs=pl.BlockSpec(memory_space=pltpu.VMEM),
            scratch_shapes=[
                pltpu.VMEM(echoes.shape, BF16),
                pltpu.VMEM(steer.shape, BF16),
                pltpu.SMEM(offsets.shape, jnp.int32),
                pltpu.VMEM(delays.shape, jnp.int32),
                pltpu.VMEM((pings, columns), jnp.int32),
                pltpu.VMEM((beams, elems, 8, bins), F32),
                pltpu.VMEM((pings, 2 * along, bins), F32),
                pltpu.VMEM((depth, columns), F32),
                pltpu.VMEM((2 * columns, 4 * depth), BF16),
                pltpu.VMEM((elems * bins, bins), BF16),
                pltpu.VMEM((beams // 2, 4 * depth, 2 * bins), BF16),
                pltpu.VMEM((8, beams, bins), F32),
                pltpu.VMEM(slots + (beams * 8, bins), BF16),
                pltpu.VMEM((len(ROUTES), 16, bins), BF16),
                pltpu.VMEM(slots + (beams * 8, bins), BF16),
                pltpu.VMEM(slots + (16, bins), BF16),
                pltpu.SemaphoreType.DMA((5,)),
                pltpu.SemaphoreType.DMA((PIECES,)),
                pltpu.SemaphoreType.DMA((PIECES,)),
                pltpu.SemaphoreType.DMA,
                pltpu.SemaphoreType.DMA,
            ],
            compiler_params=pltpu.CompilerParams(
                collective_id=0, has_side_effects=True, vmem_limit_bytes=40 * 2**20
            ),
            cost_estimate=pl.CostEstimate(
                flops=2 * columns * DMAX * depth * beams * bins,
                bytes_accessed=echoes.size * 2,
                transcendentals=0,
            ),
        )(*operands)

    placed = (
        P("ping", "elev", None, "range"),
        P("elev", None, "range"),
        P("ping"),
        P("ping", None),
        P(None, "ping"),
    )
    return jax.shard_map(
        body,
        mesh=mesh,
        in_specs=placed,
        out_specs=P(("ping", "elev"), None, "range"),
        check_vma=False,
    )
```

```python
import functools

import jax
import jax.numpy as jnp
from jax import lax
from jax.experimental import pallas as pl
from jax.experimental.pallas import tpu as pltpu
from jax.sharding import PartitionSpec as P

MESH = pl.DeviceIdType.MESH
DMAX = 8
PARTS = (32, 48, 48)
F32 = jnp.float32
BF16 = jnp.bfloat16

ROUTES = ((2, 1), (2, 0), (1, 1), (3, 1), (0, 1), (1, 0), (3, 0), (0, 0))


def target_of(ping, route):
    steps, flip = route
    y, far = ping // 2, ping % 2
    return ((y + steps) % 4) * 2 + (far + flip) % 2


def lanes(shape):
    return lax.broadcasted_iota(jnp.int32, shape, len(shape) - 1)


def kernel(
    scale, groups, ranks,
    echo_hbm, steer_hbm, off_hbm, delay_hbm, ap_hbm, out_ref,
    echo, steer, off, delay, ap, spread, table, pick_t, weight, wide, rhs, result,
    stage, stage_edge, got, got_edge,
    small_sem, share_send, share_recv, edge_send, edge_recv,
):
    ping = lax.axis_index("ping")
    rng = lax.axis_index("range")
    elev = lax.axis_index("elev")
    other = 1 - elev
    mine = 2 * ping + elev
    sides = (other, elev)
    pings, elems, along, bins = echo.shape
    beams = steer.shape[1]
    depth = pings * along

    loads = [
        pltpu.make_async_copy(src, dst, small_sem.at[i])
        for i, (src, dst) in enumerate(
            ((steer_hbm, steer), (delay_hbm, delay), (off_hbm, off), (ap_hbm, ap))
        )
    ]
    for load in loads:
        load.start()
    echo_load = pltpu.make_async_copy(echo_hbm, echo, small_sem.at[4])
    echo_load.start()

    barrier = pltpu.get_barrier_semaphore()
    for route in ROUTES:
        for side in sides:
            if route != (0, 0) or side is other:
                pl.semaphore_signal(
                    barrier, inc=1, device_id_type=MESH,
                    device_id={"ping": target_of(ping, route), "elev": side},
                )

    @pl.when(rng < groups - 1)
    def _():
        for route in ROUTES:
            for side in sides:
                pl.semaphore_signal(
                    barrier, inc=1, device_id_type=MESH,
                    device_id={"ping": target_of(ping, route), "range": rng + 1, "elev": side},
                )

    for load in loads:
        load.wait()
    for p in range(pings):
        line = jnp.broadcast_to(delay[p : p + 1, :], (2 * along, 2 * bins))
        turned = pltpu.roll(line, 0, 1, stride=1, stride_axis=0)
        table[p] = turned[:, bins:].astype(F32)
    for p in range(pings):
        valid = ap[p : p + 1, :] != 0
        picked = table[p, pl.ds(off[p], along), :]
        pick_t[pl.ds(p * along, along), :] = jnp.where(valid, picked, -1.0)
    picked = pick_t[...].T.astype(BF16)
    columns = picked.shape[0]
    one, zero = jnp.ones((), BF16), jnp.zeros((), BF16)
    starts = [sum(PARTS[:i]) for i in range(len(PARTS))]
    for start, some in zip(starts, PARTS):
        here = picked[start : start + some]
        for high in range(2):
            for low in range(4):
                weight[
                    pl.ds(2 * start + high * some, some), pl.ds(low * depth, depth)
                ] = jnp.where(here == 4 * high + low, one, zero)

    wide[...] = jnp.zeros_like(wide)
    lane = lanes((beams, bins))
    row = lax.broadcasted_iota(jnp.int32, (beams, bins), 0)
    for e in range(elems):
        rows = steer[e].astype(F32)
        for b in range(beams):
            spread[b, e] = jnp.broadcast_to(rows[b : b + 1], (8, bins))
        moved = pltpu.roll(jnp.where(lane < 8, rows, 0.0), 8, 1, stride=16, stride_axis=0)
        line = jnp.sum(moved, axis=0, keepdims=True)
        diag = jnp.where(lane % 16 - 8 == row, line, 0.0)
        diag = jnp.concatenate([diag, jnp.zeros_like(diag)], axis=0)
        wide[pl.ds(e * bins, 16), :] = diag.astype(BF16)

    def later(values, count):
        moved = pltpu.roll(values, bins - count, 1)
        return jnp.where(lanes(values.shape) < bins - count, moved, jnp.zeros((), values.dtype))

    echo_load.wait()

    flat = [jnp.concatenate([echo[p, e] for e in range(elems)], axis=1) for p in range(pings)]
    heads = jnp.dot(jnp.concatenate(flat, axis=0), wide[...], preferred_element_type=F32)
    heads = heads.astype(BF16)
    for low in range(4):
        moved = pltpu.roll(heads, bins - low, 1) if low else heads
        rhs[pl.ds(low * depth, depth), pl.ds(beams * bins, bins)] = moved

    def make_beam(b):
        rows = []
        for p in range(pings):
            total = None
            for e in range(elems):
                line = jnp.concatenate([spread[b, e]] * (along // 8), axis=0)
                term = echo[p, e].astype(F32) * line
                total = term if total is None else total + term
            rows.append(total.astype(BF16))
        beam = jnp.concatenate(rows, axis=0)
        place = pl.ds(b * bins, bins)
        rhs[pl.ds(0, depth), place] = beam
        for low in range(1, 4):
            rhs[pl.ds(low * depth, depth), place] = later(beam, low)

    def project(start, some):
        picks = weight[pl.ds(2 * start, 2 * some), :]
        prod = jnp.dot(picks, rhs[...], preferred_element_type=F32)
        images = [
            prod[:some, b * bins : (b + 1) * bins]
            + later(prod[some:, b * bins : (b + 1) * bins], 4)
            for b in range(beams)
        ]
        edge = prod[:some, beams * bins :] + pltpu.roll(prod[some:, beams * bins :], bins - 4, 1)
        for j in range(some // 8):
            for b in range(0, beams, 2):
                rows = [image[8 * j : 8 * j + 8] for image in images[b : b + 2]]
                block = start // 8 + j
                stage[block, pl.ds(8 * b, 16), :] = jnp.concatenate(rows, axis=0).astype(BF16)
        for i in range(some // 16):
            stage_edge[start // 16 + i] = edge[16 * i : 16 * i + 16].astype(BF16)

    def send_share(target, core):
        share = pltpu.make_async_remote_copy(
            src_ref=stage.at[2 * target + core],
            dst_ref=got.at[mine],
            send_sem=share_send,
            recv_sem=share_recv,
            device_id={"ping": jnp.int32(target), "elev": core},
            device_id_type=MESH,
        )
        if core is elev:
            pl.when(ping != target)(share.start)
        else:
            share.start()

    def send_edges(target):
        for core in sides:
            pltpu.make_async_remote_copy(
                src_ref=stage_edge.at[target],
                dst_ref=got_edge.at[mine],
                send_sem=edge_send,
                recv_sem=edge_recv,
                device_id={"ping": jnp.int32(target), "range": rng - 1, "elev": core},
                device_id_type=MESH,
            ).start()

    def send(start, some):
        for target in range(start // 16, (start + some) // 16):
            for core in sides:
                send_share(target, core)
            pl.when(rng > 0)(functools.partial(send_edges, target))

    for b in range(beams):
        make_beam(b)
    for start, some in zip(starts, PARTS):
        project(start, some)
        if start == 0:
            pl.semaphore_wait(
                barrier, 2 * len(ROUTES) - 1 + jnp.where(rng > 0, 2 * len(ROUTES), 0)
            )
        send(start, some)

    every = pl.ds(0, 2 * ranks - 1)
    all_shares = pltpu.make_async_remote_copy(
        src_ref=stage.at[every],
        dst_ref=got.at[every],
        send_sem=share_send,
        recv_sem=share_recv,
        device_id={"elev": other},
        device_id_type=MESH,
    )
    all_edges = pltpu.make_async_remote_copy(
        src_ref=got_edge,
        dst_ref=got_edge,
        send_sem=edge_send,
        recv_sem=edge_recv,
        device_id={"elev": other},
        device_id_type=MESH,
    )

    @pl.when(rng < groups - 1)
    def _():
        all_edges.wait_recv()

    @pl.when(rng == groups - 1)
    def _():
        got_edge[...] = jnp.zeros_like(got_edge)

    edge = jnp.zeros((16, bins), F32)
    for i in range(2 * len(ROUTES)):
        edge = edge + got_edge[i].astype(F32)
    edge = jnp.where(elev == 0, edge[:8], edge[8:])
    got[mine] = stage[mine]
    all_shares.wait_recv()
    total = jnp.zeros((beams * 8, bins), F32)
    for i in range(2 * ranks):
        total = total + got[i].astype(F32)
    for b in range(beams):
        moved = pltpu.roll(edge, (2 * bins - 8 - 16 * b) % bins, 1)
        end = jnp.where(lane >= bins - 8, moved, 0.0)
        result[:, b, :] = (total[8 * b : 8 * b + 8] + end) * scale
    out_ref[...] = result[...].astype(BF16)

    all_shares.wait_send()

    @pl.when(rng > 0)
    def _():
        all_edges.wait_send()


def solution(mesh):
    groups = mesh.shape["range"]
    ranks = mesh.shape["ping"]

    def body(echoes, steer, offsets, delays, aperture):
        pings, elems, along, bins = echoes.shape
        beams = steer.shape[1]
        columns = aperture.shape[0]
        depth = pings * along
        scale = float(ranks * pings * along) ** (-0.5)
        slots = (2 * len(ROUTES),)
        operands = (echoes, steer, offsets, delays, jnp.transpose(aperture))
        operands = [pltpu.with_memory_space_constraint(v, pltpu.HBM) for v in operands]
        return pl.pallas_call(
            functools.partial(kernel, scale, groups, ranks),
            out_shape=jax.ShapeDtypeStruct((8, beams, bins), BF16),
            in_specs=[pl.BlockSpec(memory_space=pltpu.HBM)] * 5,
            out_specs=pl.BlockSpec(memory_space=pltpu.VMEM),
            scratch_shapes=[
                pltpu.VMEM(echoes.shape, BF16),
                pltpu.VMEM(steer.shape, BF16),
                pltpu.SMEM(offsets.shape, jnp.int32),
                pltpu.VMEM(delays.shape, jnp.int32),
                pltpu.VMEM((pings, columns), jnp.int32),
                pltpu.VMEM((beams, elems, 8, bins), F32),
                pltpu.VMEM((pings, 2 * along, bins), F32),
                pltpu.VMEM((depth, columns), F32),
                pltpu.VMEM((2 * columns, 4 * depth), BF16),
                pltpu.VMEM((elems * bins, bins), BF16),
                pltpu.VMEM((4 * depth, (beams + 1) * bins), BF16),
                pltpu.VMEM((8, beams, bins), F32),
                pltpu.VMEM(slots + (beams * 8, bins), BF16),
                pltpu.VMEM((len(ROUTES), 16, bins), BF16),
                pltpu.VMEM(slots + (beams * 8, bins), BF16),
                pltpu.VMEM(slots + (16, bins), BF16),
                pltpu.SemaphoreType.DMA((5,)),
                pltpu.SemaphoreType.DMA,
                pltpu.SemaphoreType.DMA,
                pltpu.SemaphoreType.DMA,
                pltpu.SemaphoreType.DMA,
            ],
            compiler_params=pltpu.CompilerParams(
                collective_id=0, has_side_effects=True, vmem_limit_bytes=40 * 2**20
            ),
            cost_estimate=pl.CostEstimate(
                flops=2 * columns * DMAX * depth * beams * bins,
                bytes_accessed=echoes.size * 2,
                transcendentals=0,
            ),
        )(*operands)

    placed = (
        P("ping", "elev", None, "range"),
        P("elev", None, "range"),
        P("ping"),
        P("ping", None),
        P(None, "ping"),
    )
    return jax.shard_map(
        body,
        mesh=mesh,
        in_specs=placed,
        out_specs=P(("ping", "elev"), None, "range"),
        check_vma=False,
    )
```

```python
import functools

import jax
import jax.numpy as jnp
from jax import lax
from jax.experimental import pallas as pl
from jax.experimental.pallas import tpu as pltpu
from jax.sharding import PartitionSpec as P

MESH = pl.DeviceIdType.MESH
DMAX = 8
PARTS = (32, 96)
F32 = jnp.float32
BF16 = jnp.bfloat16

ROUTES = ((2, 1), (2, 0), (1, 1), (3, 1), (0, 1), (1, 0), (3, 0), (0, 0))


def target_of(ping, route):
    steps, flip = route
    y, far = ping // 2, ping % 2
    return ((y + steps) % 4) * 2 + (far + flip) % 2


def lanes(shape):
    return lax.broadcasted_iota(jnp.int32, shape, len(shape) - 1)


def kernel(
    scale, groups, ranks,
    echo_hbm, steer_hbm, off_hbm, delay_hbm, ap_hbm, out_ref,
    echo, steer, off, delay, ap, spread, table, pick_t, weight, wide, rhs, result,
    stage, swapped, summed, got, got_edge,
    small_sem, share_send, share_recv, edge_send, edge_recv, swap_send, swap_recv,
):
    ping = lax.axis_index("ping")
    rng = lax.axis_index("range")
    elev = lax.axis_index("elev")
    other = 1 - elev
    sides = (other, elev)
    pings, elems, along, bins = echo.shape
    beams = steer.shape[1]
    depth = pings * along

    loads = [
        pltpu.make_async_copy(src, dst, small_sem.at[i])
        for i, (src, dst) in enumerate(
            ((steer_hbm, steer), (delay_hbm, delay), (off_hbm, off), (ap_hbm, ap))
        )
    ]
    for load in loads:
        load.start()
    echo_load = pltpu.make_async_copy(echo_hbm, echo, small_sem.at[4])
    echo_load.start()

    barrier = pltpu.get_barrier_semaphore()
    pl.semaphore_signal(
        barrier, inc=1, device_id={"elev": other}, device_id_type=MESH
    )
    for route in ROUTES[:-1]:
        pl.semaphore_signal(
            barrier, inc=1, device_id={"ping": target_of(ping, route)}, device_id_type=MESH
        )

    @pl.when(rng < groups - 1)
    def _():
        for route in ROUTES:
            pl.semaphore_signal(
                barrier, inc=1, device_id_type=MESH,
                device_id={"ping": target_of(ping, route), "range": rng + 1},
            )

    for load in loads:
        load.wait()
    for p in range(pings):
        line = jnp.broadcast_to(delay[p : p + 1, :], (2 * along, 2 * bins))
        turned = pltpu.roll(line, 0, 1, stride=1, stride_axis=0)
        table[p] = turned[:, bins:].astype(F32)
    for p in range(pings):
        valid = ap[p : p + 1, :] != 0
        picked = table[p, pl.ds(off[p], along), :]
        pick_t[pl.ds(p * along, along), :] = jnp.where(valid, picked, -1.0)
    picked = pick_t[...].T.astype(BF16)
    columns = picked.shape[0]
    one, zero = jnp.ones((), BF16), jnp.zeros((), BF16)
    starts = [sum(PARTS[:i]) for i in range(len(PARTS))]
    for start, some in zip(starts, PARTS):
        here = picked[start : start + some]
        for high in range(2):
            for low in range(4):
                weight[
                    pl.ds(2 * start + high * some, some), pl.ds(low * depth, depth)
                ] = jnp.where(here == 4 * high + low, one, zero)

    wide[...] = jnp.zeros_like(wide)
    lane = lanes((beams, bins))
    row = lax.broadcasted_iota(jnp.int32, (beams, bins), 0)
    for e in range(elems):
        rows = steer[e].astype(F32)
        for b in range(beams):
            spread[b, e] = jnp.broadcast_to(rows[b : b + 1], (8, bins))
        moved = pltpu.roll(jnp.where(lane < 8, rows, 0.0), 8, 1, stride=16, stride_axis=0)
        line = jnp.sum(moved, axis=0, keepdims=True)
        diag = jnp.where(lane % 16 - 8 == row, line, 0.0)
        diag = jnp.concatenate([diag, jnp.zeros_like(diag)], axis=0)
        wide[pl.ds(e * bins, 16), :] = diag.astype(BF16)

    def later(values, count):
        moved = pltpu.roll(values, bins - count, 1)
        return jnp.where(lanes(values.shape) < bins - count, moved, jnp.zeros((), values.dtype))

    echo_load.wait()

    store = {}

    class Put:
        def __init__(self, key):
            self.key = key

        def __setitem__(self, _, value):
            store[self.key] = value

    def RHS(b, low):
        return Put((b, low))

    def PAIR(q):
        return jnp.concatenate([jnp.concatenate([store[2*q,l] for l in range(4)],axis=0), jnp.concatenate([store[2*q+1,l] for l in range(4)],axis=0)],axis=1)

    def HEADS():
        return jnp.concatenate([store[beams,l] for l in range(4)],axis=0)

    flat = [jnp.concatenate([echo[p, e] for e in range(elems)], axis=1) for p in range(pings)]
    flat = jnp.concatenate(flat, axis=0)

    def make_heads():
        heads = jnp.dot(flat, wide[...], preferred_element_type=F32).astype(BF16)
        for low in range(4):
            moved = pltpu.roll(heads, bins - low, 1) if low else heads
            RHS(beams, low)[...] = moved

    def make_beam(b):
        rows = []
        for p in range(pings):
            total = None
            for e in range(elems):
                line = jnp.concatenate([spread[b, e]] * (along // 8), axis=0)
                term = echo[p, e].astype(F32) * line
                total = term if total is None else total + term
            rows.append(total.astype(BF16))
        beam = jnp.concatenate(rows, axis=0)
        RHS(b, 0)[...] = beam
        for low in range(1, 4):
            RHS(b, low)[...] = later(beam, low)

    def project(start, some, b):
        picks = weight[pl.ds(2 * start, 2 * some), :]
        prod = jnp.dot(picks, PAIR(b // 2), preferred_element_type=F32)
        images = [
            prod[:some, c * bins : (c + 1) * bins]
            + later(prod[some:, c * bins : (c + 1) * bins], 4)
            for c in range(2)
        ]
        for j in range(some // 8):
            rows = [image[8 * j : 8 * j + 8] for image in images]
            stage[start // 16 + j // 2, j % 2, pl.ds(8 * b, 16), :] = jnp.concatenate(rows, axis=0).astype(BF16)

    def project_edge(start, some):
        picks = weight[pl.ds(2 * start, 2 * some), :]
        prod = jnp.dot(picks, HEADS(), preferred_element_type=F32)
        edge = prod[:some] + pltpu.roll(prod[some:], bins - 4, 1)
        for i in range(some // 16):
            for c in range(2):
                rows = edge[16 * i + 8 * c : 16 * i + 8 * c + 8]
                rows = jnp.concatenate([rows, jnp.zeros_like(rows)], axis=0).astype(BF16)
                stage[start // 16 + i, c, pl.ds(8 * beams, 16), :] = rows

    def swap_of(part):
        places = pl.ds(starts[part] // 16, PARTS[part] // 16)
        return pltpu.make_async_remote_copy(
            src_ref=stage.at[places, other],
            dst_ref=swapped.at[places],
            send_sem=swap_send.at[part],
            recv_sem=swap_recv.at[part],
            device_id={"elev": other},
            device_id_type=MESH,
        )

    def combine(part):
        for target in range(starts[part] // 16, (starts[part] + PARTS[part]) // 16):
            both = stage[target, elev].astype(F32) + swapped[target].astype(F32)
            summed[target] = both.astype(BF16)

    def send(part):
        for target in range(starts[part] // 16, (starts[part] + PARTS[part]) // 16):
            share = pltpu.make_async_remote_copy(
                src_ref=summed.at[target, pl.ds(0, 8 * beams)],
                dst_ref=got.at[ping],
                send_sem=share_send,
                recv_sem=share_recv,
                device_id={"ping": jnp.int32(target)},
                device_id_type=MESH,
            )
            pl.when(ping != target)(share.start)
            edge = pltpu.make_async_remote_copy(
                src_ref=summed.at[target, pl.ds(8 * beams, 16)],
                dst_ref=got_edge.at[ping],
                send_sem=edge_send,
                recv_sem=edge_recv,
                device_id={"ping": jnp.int32(target), "range": rng - 1},
                device_id_type=MESH,
            )
            pl.when(rng > 0)(edge.start)

    make_heads()
    for b in range(beams):
        make_beam(b)
    for part, (start, some) in enumerate(zip(starts, PARTS)):
        for b in range(0, beams, 2):
            project(start, some, b)
        project_edge(start, some)
        if part == 0:
            pl.semaphore_wait(barrier, ranks + jnp.where(rng > 0, ranks, 0))
        swap_of(part).start()
    for part in range(len(PARTS)):
        swap_of(part).wait_recv()
        combine(part)
        send(part)

    every = pl.ds(0, ranks - 1)
    all_shares = pltpu.make_async_remote_copy(
        src_ref=got.at[every],
        dst_ref=got.at[every],
        send_sem=share_send,
        recv_sem=share_recv,
        device_id={"elev": other},
        device_id_type=MESH,
    )
    all_edges = pltpu.make_async_remote_copy(
        src_ref=got_edge,
        dst_ref=got_edge,
        send_sem=edge_send,
        recv_sem=edge_recv,
        device_id={"elev": other},
        device_id_type=MESH,
    )

    @pl.when(rng < groups - 1)
    def _():
        all_edges.wait_recv()

    @pl.when(rng == groups - 1)
    def _():
        got_edge[...] = jnp.zeros_like(got_edge)

    edge = jnp.zeros((16, bins), F32)
    for i in range(ranks):
        edge = edge + got_edge[i].astype(F32)
    edge = edge[:8]
    got[ping] = summed[ping, pl.ds(0, 8 * beams), :]
    all_shares.wait_recv()
    total = jnp.zeros((beams * 8, bins), F32)
    for i in range(ranks):
        total = total + got[i].astype(F32)
    for b in range(beams):
        moved = pltpu.roll(edge, (2 * bins - 8 - 16 * b) % bins, 1)
        end = jnp.where(lane >= bins - 8, moved, 0.0)
        result[:, b, :] = (total[8 * b : 8 * b + 8] + end) * scale
    out_ref[...] = result[...].astype(BF16)

    all_shares.wait_send()
    for part in range(len(PARTS)):
        swap_of(part).wait_send()

    @pl.when(rng > 0)
    def _():
        all_edges.wait_send()


def solution(mesh):
    groups = mesh.shape["range"]
    ranks = mesh.shape["ping"]

    def body(echoes, steer, offsets, delays, aperture):
        pings, elems, along, bins = echoes.shape
        beams = steer.shape[1]
        columns = aperture.shape[0]
        depth = pings * along
        scale = float(ranks * pings * along) ** (-0.5)
        operands = (echoes, steer, offsets, delays, jnp.transpose(aperture))
        operands = [pltpu.with_memory_space_constraint(v, pltpu.HBM) for v in operands]
        return pl.pallas_call(
            functools.partial(kernel, scale, groups, ranks),
            out_shape=jax.ShapeDtypeStruct((8, beams, bins), BF16),
            in_specs=[pl.BlockSpec(memory_space=pltpu.HBM)] * 5,
            out_specs=pl.BlockSpec(memory_space=pltpu.VMEM),
            scratch_shapes=[
                pltpu.VMEM(echoes.shape, BF16),
                pltpu.VMEM(steer.shape, BF16),
                pltpu.SMEM(offsets.shape, jnp.int32),
                pltpu.VMEM(delays.shape, jnp.int32),
                pltpu.VMEM((pings, columns), jnp.int32),
                pltpu.VMEM((beams, elems, 8, bins), F32),
                pltpu.VMEM((pings, 2 * along, bins), F32),
                pltpu.VMEM((depth, columns), F32),
                pltpu.VMEM((2 * columns, 4 * depth), BF16),
                pltpu.VMEM((elems * bins, bins), BF16),
                pltpu.VMEM((4 * depth, (beams + 1) * bins), BF16),
                pltpu.VMEM((8, beams, bins), F32),
                pltpu.VMEM((ranks, 2, beams * 8 + 16, bins), BF16),
                pltpu.VMEM((ranks, beams * 8 + 16, bins), BF16),
                pltpu.VMEM((ranks, beams * 8 + 16, bins), BF16),
                pltpu.VMEM((ranks, beams * 8, bins), BF16),
                pltpu.VMEM((ranks, 16, bins), BF16),
                pltpu.SemaphoreType.DMA((5,)),
                pltpu.SemaphoreType.DMA,
                pltpu.SemaphoreType.DMA,
                pltpu.SemaphoreType.DMA,
                pltpu.SemaphoreType.DMA,
                pltpu.SemaphoreType.DMA((len(PARTS),)),
                pltpu.SemaphoreType.DMA((len(PARTS),)),
            ],
            compiler_params=pltpu.CompilerParams(
                collective_id=0, has_side_effects=True, vmem_limit_bytes=40 * 2**20
            ),
            cost_estimate=pl.CostEstimate(
                flops=2 * columns * DMAX * depth * beams * bins,
                bytes_accessed=echoes.size * 2,
                transcendentals=0,
            ),
        )(*operands)

    placed = (
        P("ping", "elev", None, "range"),
        P("elev", None, "range"),
        P("ping"),
        P("ping", None),
        P(None, "ping"),
    )
    return jax.shard_map(
        body,
        mesh=mesh,
        in_specs=placed,
        out_specs=P(("ping", "elev"), None, "range"),
        check_vma=False,
    )
```

```python
import functools

import jax
import jax.numpy as jnp
from jax import lax
from jax.experimental import pallas as pl
from jax.experimental.pallas import tpu as pltpu
from jax.sharding import PartitionSpec as P

MESH = pl.DeviceIdType.MESH
DMAX = 8
DIRECT = 3
PARTS = (128,)
F32 = jnp.float32
BF16 = jnp.bfloat16

ROUTES = ((2, 1), (2, 0), (1, 1), (3, 1), (0, 1), (1, 0), (3, 0), (0, 0))


def target_of(ping, route):
    steps, flip = route
    y, far = ping // 2, ping % 2
    return ((y + steps) % 4) * 2 + (far + flip) % 2


def lanes(shape):
    return lax.broadcasted_iota(jnp.int32, shape, len(shape) - 1)


def kernel(
    scale, groups, ranks,
    echo_hbm, steer_hbm, off_hbm, delay_hbm, ap_hbm, out_ref,
    echo, steer, off, delay, ap, spread, table, pick_t, weight, wide, rhs, result,
    stage, swapped, summed, got, got_edge,
    small_sem, share_send, share_recv, edge_send, edge_recv, swap_send, swap_recv,
):
    ping = lax.axis_index("ping")
    rng = lax.axis_index("range")
    elev = lax.axis_index("elev")
    other = 1 - elev
    sides = (other, elev)
    pings, elems, along, bins = echo.shape
    beams = steer.shape[1]
    depth = pings * along

    loads = [
        pltpu.make_async_copy(src, dst, small_sem.at[i])
        for i, (src, dst) in enumerate(
            ((steer_hbm, steer), (delay_hbm, delay), (off_hbm, off), (ap_hbm, ap))
        )
    ]
    for load in loads:
        load.start()
    echo_load = pltpu.make_async_copy(echo_hbm, echo, small_sem.at[4])
    echo_load.start()

    barrier = pltpu.get_barrier_semaphore()
    pl.semaphore_signal(
        barrier, inc=1, device_id={"elev": other}, device_id_type=MESH
    )
    for route in ROUTES[:-1]:
        pl.semaphore_signal(
            barrier, inc=1, device_id={"ping": target_of(ping, route)}, device_id_type=MESH
        )

    @pl.when(ping < DIRECT)
    def _():
        for route in ROUTES[:-1]:
            pl.semaphore_signal(
                barrier, inc=1, device_id_type=MESH,
                device_id={"ping": target_of(ping, route), "elev": other},
            )

    @pl.when(rng < groups - 1)
    def _():
        for route in ROUTES:
            pl.semaphore_signal(
                barrier, inc=1, device_id_type=MESH,
                device_id={"ping": target_of(ping, route), "range": rng + 1},
            )

    @pl.when((rng < groups - 1) & (ping < DIRECT))
    def _():
        for route in ROUTES:
            pl.semaphore_signal(
                barrier, inc=1, device_id_type=MESH,
                device_id={"ping": target_of(ping, route), "range": rng + 1, "elev": other},
            )

    for load in loads:
        load.wait()
    for p in range(pings):
        line = jnp.broadcast_to(delay[p : p + 1, :], (2 * along, 2 * bins))
        turned = pltpu.roll(line, 0, 1, stride=1, stride_axis=0)
        table[p] = turned[:, bins:].astype(F32)
    for p in range(pings):
        valid = ap[p : p + 1, :] != 0
        picked = table[p, pl.ds(off[p], along), :]
        pick_t[pl.ds(p * along, along), :] = jnp.where(valid, picked, -1.0)
    picked = pick_t[...].T.astype(BF16)
    columns = picked.shape[0]
    one, zero = jnp.ones((), BF16), jnp.zeros((), BF16)
    starts = [sum(PARTS[:i]) for i in range(len(PARTS))]
    for start, some in zip(starts, PARTS):
        here = picked[start : start + some]
        for high in range(2):
            for low in range(4):
                weight[
                    pl.ds(2 * start + high * some, some), pl.ds(low * depth, depth)
                ] = jnp.where(here == 4 * high + low, one, zero)

    wide[...] = jnp.zeros_like(wide)
    lane = lanes((beams, bins))
    row = lax.broadcasted_iota(jnp.int32, (beams, bins), 0)
    for e in range(elems):
        rows = steer[e].astype(F32)
        for b in range(beams):
            spread[b, e] = jnp.broadcast_to(rows[b : b + 1], (8, bins))
        moved = pltpu.roll(jnp.where(lane < 8, rows, 0.0), 8, 1, stride=16, stride_axis=0)
        line = jnp.sum(moved, axis=0, keepdims=True)
        diag = jnp.where(lane % 16 - 8 == row, line, 0.0)
        diag = jnp.concatenate([diag, jnp.zeros_like(diag)], axis=0)
        wide[pl.ds(e * bins, 16), :] = diag.astype(BF16)

    def later(values, count):
        moved = pltpu.roll(values, bins - count, 1)
        return jnp.where(lanes(values.shape) < bins - count, moved, jnp.zeros((), values.dtype))

    echo_load.wait()

    store = {}

    class Put:
        def __init__(self, key):
            self.key = key

        def __setitem__(self, _, value):
            store[self.key] = value

    def RHS(b, low):
        return Put((b, low))

    def PAIR(q):
        return jnp.concatenate([jnp.concatenate([store[2*q,l] for l in range(4)],axis=0), jnp.concatenate([store[2*q+1,l] for l in range(4)],axis=0)],axis=1)

    def HEADS():
        return jnp.concatenate([store[beams,l] for l in range(4)],axis=0)

    flat = [jnp.concatenate([echo[p, e] for e in range(elems)], axis=1) for p in range(pings)]
    flat = jnp.concatenate(flat, axis=0)

    def make_heads():
        heads = jnp.dot(flat, wide[...], preferred_element_type=F32).astype(BF16)
        for low in range(4):
            moved = pltpu.roll(heads, bins - low, 1) if low else heads
            RHS(beams, low)[...] = moved

    def make_beam(b):
        rows = []
        for p in range(pings):
            total = None
            for e in range(elems):
                line = jnp.concatenate([spread[b, e]] * (along // 8), axis=0)
                term = echo[p, e].astype(F32) * line
                total = term if total is None else total + term
            rows.append(total.astype(BF16))
        beam = jnp.concatenate(rows, axis=0)
        RHS(b, 0)[...] = beam
        for low in range(1, 4):
            RHS(b, low)[...] = later(beam, low)

    def project(start, some, b):
        picks = weight[pl.ds(2 * start, 2 * some), :]
        prod = jnp.dot(picks, PAIR(b // 2), preferred_element_type=F32)
        images = [
            prod[:some, c * bins : (c + 1) * bins]
            + later(prod[some:, c * bins : (c + 1) * bins], 4)
            for c in range(2)
        ]
        for j in range(some // 8):
            rows = [image[8 * j : 8 * j + 8] for image in images]
            stage[start // 16 + j // 2, j % 2, pl.ds(8 * b, 16), :] = jnp.concatenate(rows, axis=0).astype(BF16)

    def project_edge(start, some):
        picks = weight[pl.ds(2 * start, 2 * some), :]
        prod = jnp.dot(picks, HEADS(), preferred_element_type=F32)
        edge = prod[:some] + pltpu.roll(prod[some:], bins - 4, 1)
        for i in range(some // 16):
            for c in range(2):
                rows = edge[16 * i + 8 * c : 16 * i + 8 * c + 8]
                rows = jnp.concatenate([rows, jnp.zeros_like(rows)], axis=0).astype(BF16)
                stage[start // 16 + i, c, pl.ds(8 * beams, 16), :] = rows

    rest = pl.ds(DIRECT, ranks - DIRECT)
    swap = pltpu.make_async_remote_copy(
        src_ref=stage.at[rest, other],
        dst_ref=swapped.at[rest],
        send_sem=swap_send,
        recv_sem=swap_recv,
        device_id={"elev": other},
        device_id_type=MESH,
    )

    def share(source, slot, target, core):
        return pltpu.make_async_remote_copy(
            src_ref=source.at[pl.ds(0, 8 * beams)],
            dst_ref=got.at[slot],
            send_sem=share_send,
            recv_sem=share_recv,
            device_id={"ping": jnp.int32(target), "elev": core},
            device_id_type=MESH,
        )

    def spill(source, slot, target, core):
        return pltpu.make_async_remote_copy(
            src_ref=source.at[pl.ds(8 * beams, 16)],
            dst_ref=got_edge.at[slot],
            send_sem=edge_send,
            recv_sem=edge_recv,
            device_id={"ping": jnp.int32(target), "range": rng - 1, "elev": core},
            device_id_type=MESH,
        )

    def send_direct():
        slot = 2 * ping + elev
        for target in range(DIRECT):
            share(stage.at[target, other], slot, target, other).start()
            pl.when(ping != target)(share(stage.at[target, elev], slot, target, elev).start)

        @pl.when(rng > 0)
        def _():
            for target in range(DIRECT):
                for core in sides:
                    spill(stage.at[target, core], slot, target, core).start()

    def send_summed():
        for target in range(DIRECT):
            summed[target] = stage[target, elev]
        for target in range(DIRECT, ranks):
            both = stage[target, elev].astype(F32) + swapped[target].astype(F32)
            summed[target] = both.astype(BF16)
        for target in range(DIRECT, ranks):
            pl.when(ping != target)(share(summed.at[target], ping, target, elev).start)

        @pl.when(rng > 0)
        def _():
            for target in range(DIRECT, ranks):
                spill(summed.at[target], ping, target, elev).start()

    make_heads()
    for b in range(beams):
        make_beam(b)
    for b in range(0, beams, 2):
        project(0, columns, b)
    project_edge(0, columns)
    pl.semaphore_wait(
        barrier,
        ranks - 1 + DIRECT + jnp.where(ping < DIRECT, 0, 1) + jnp.where(rng > 0, ranks + DIRECT, 0),
    )
    send_direct()
    swap.start()
    swap.wait_recv()
    send_summed()

    def shares_of(count):
        return pltpu.make_async_remote_copy(
            src_ref=got.at[pl.ds(0, count)],
            dst_ref=got.at[pl.ds(0, count)],
            send_sem=share_send,
            recv_sem=share_recv,
            device_id={"elev": other},
            device_id_type=MESH,
        )

    def spills_of(count):
        return pltpu.make_async_remote_copy(
            src_ref=got_edge.at[pl.ds(0, count)],
            dst_ref=got_edge.at[pl.ds(0, count)],
            send_sem=edge_send,
            recv_sem=edge_recv,
            device_id={"elev": other},
            device_id_type=MESH,
        )

    direct = ping < DIRECT
    pl.when((rng < groups - 1) & direct)(spills_of(2 * ranks).wait_recv)
    pl.when((rng < groups - 1) & (ping >= DIRECT))(spills_of(ranks).wait_recv)

    @pl.when(rng == groups - 1)
    def _():
        got_edge[...] = jnp.zeros_like(got_edge)

    edge = jnp.zeros((16, bins), F32)
    for i in range(2 * ranks):
        part = got_edge[i].astype(F32)
        edge = edge + (part if i < ranks else jnp.where(direct, part, 0.0))
    edge = edge[:8]
    got[jnp.where(direct, 2 * ping + elev, ping)] = summed[ping, pl.ds(0, 8 * beams), :]
    pl.when(direct)(shares_of(2 * ranks - 1).wait_recv)
    pl.when(ping >= DIRECT)(shares_of(ranks - 1).wait_recv)
    total = jnp.zeros((beams * 8, bins), F32)
    for i in range(2 * ranks):
        part = got[i].astype(F32)
        total = total + (part if i < ranks else jnp.where(direct, part, 0.0))
    for b in range(beams):
        moved = pltpu.roll(edge, (2 * bins - 8 - 16 * b) % bins, 1)
        end = jnp.where(lane >= bins - 8, moved, 0.0)
        result[:, b, :] = (total[8 * b : 8 * b + 8] + end) * scale
    out_ref[...] = result[...].astype(BF16)

    shares_of(ranks - 1 + DIRECT).wait_send()
    swap.wait_send()
    pl.when(rng > 0)(spills_of(ranks + DIRECT).wait_send)


def solution(mesh):
    groups = mesh.shape["range"]
    ranks = mesh.shape["ping"]

    def body(echoes, steer, offsets, delays, aperture):
        pings, elems, along, bins = echoes.shape
        beams = steer.shape[1]
        columns = aperture.shape[0]
        depth = pings * along
        scale = float(ranks * pings * along) ** (-0.5)
        operands = (echoes, steer, offsets, delays, jnp.transpose(aperture))
        operands = [pltpu.with_memory_space_constraint(v, pltpu.HBM) for v in operands]
        return pl.pallas_call(
            functools.partial(kernel, scale, groups, ranks),
            out_shape=jax.ShapeDtypeStruct((8, beams, bins), BF16),
            in_specs=[pl.BlockSpec(memory_space=pltpu.HBM)] * 5,
            out_specs=pl.BlockSpec(memory_space=pltpu.VMEM),
            scratch_shapes=[
                pltpu.VMEM(echoes.shape, BF16),
                pltpu.VMEM(steer.shape, BF16),
                pltpu.SMEM(offsets.shape, jnp.int32),
                pltpu.VMEM(delays.shape, jnp.int32),
                pltpu.VMEM((pings, columns), jnp.int32),
                pltpu.VMEM((beams, elems, 8, bins), F32),
                pltpu.VMEM((pings, 2 * along, bins), F32),
                pltpu.VMEM((depth, columns), F32),
                pltpu.VMEM((2 * columns, 4 * depth), BF16),
                pltpu.VMEM((elems * bins, bins), BF16),
                pltpu.VMEM((4 * depth, (beams + 1) * bins), BF16),
                pltpu.VMEM((8, beams, bins), F32),
                pltpu.VMEM((ranks, 2, beams * 8 + 16, bins), BF16),
                pltpu.VMEM((ranks, beams * 8 + 16, bins), BF16),
                pltpu.VMEM((ranks, beams * 8 + 16, bins), BF16),
                pltpu.VMEM((2 * ranks, beams * 8, bins), BF16),
                pltpu.VMEM((2 * ranks, 16, bins), BF16),
                pltpu.SemaphoreType.DMA((5,)),
                pltpu.SemaphoreType.DMA,
                pltpu.SemaphoreType.DMA,
                pltpu.SemaphoreType.DMA,
                pltpu.SemaphoreType.DMA,
                pltpu.SemaphoreType.DMA,
                pltpu.SemaphoreType.DMA,
            ],
            compiler_params=pltpu.CompilerParams(
                collective_id=0, has_side_effects=True, vmem_limit_bytes=40 * 2**20
            ),
            cost_estimate=pl.CostEstimate(
                flops=2 * columns * DMAX * depth * beams * bins,
                bytes_accessed=echoes.size * 2,
                transcendentals=0,
            ),
        )(*operands)

    placed = (
        P("ping", "elev", None, "range"),
        P("elev", None, "range"),
        P("ping"),
        P("ping", None),
        P(None, "ping"),
    )
    return jax.shard_map(
        body,
        mesh=mesh,
        in_specs=placed,
        out_specs=P(("ping", "elev"), None, "range"),
        check_vma=False,
    )
```

```python
import functools

import jax
import jax.numpy as jnp
from jax import lax
from jax.experimental import pallas as pl
from jax.experimental.pallas import tpu as pltpu
from jax.sharding import PartitionSpec as P

MESH = pl.DeviceIdType.MESH
DMAX = 8
DIRECT = 3
PARTS = (128,)
F32 = jnp.float32
BF16 = jnp.bfloat16

ROUTES = ((2, 1), (2, 0), (1, 1), (3, 1), (0, 1), (1, 0), (3, 0), (0, 0))


def target_of(ping, route):
    steps, flip = route
    y, far = ping // 2, ping % 2
    return ((y + steps) % 4) * 2 + (far + flip) % 2


def lanes(shape):
    return lax.broadcasted_iota(jnp.int32, shape, len(shape) - 1)


def kernel(
    scale, groups, ranks,
    echo_hbm, steer_hbm, off_hbm, delay_hbm, ap_hbm, out_ref,
    echo, steer, off, delay, ap, spread, table, pick_t, weight, wide, rhs, result,
    stage, swapped, summed, got, got_edge,
    small_sem, share_send, share_recv, edge_send, edge_recv, swap_send, swap_recv,
):
    ping = lax.axis_index("ping")
    rng = lax.axis_index("range")
    elev = lax.axis_index("elev")
    other = 1 - elev
    sides = (other, elev)
    pings, elems, along, bins = echo.shape
    beams = steer.shape[1]
    depth = pings * along

    loads = [
        pltpu.make_async_copy(src, dst, small_sem.at[i])
        for i, (src, dst) in enumerate(
            ((steer_hbm, steer), (delay_hbm, delay), (off_hbm, off), (ap_hbm, ap))
        )
    ]
    for load in loads:
        load.start()
    each = pings // 2
    echo_loads = [
        pltpu.make_async_copy(
            echo_hbm.at[pl.ds(i * each, each)], echo.at[pl.ds(i * each, each)], small_sem.at[4 + i]
        )
        for i in range(2)
    ]
    for load in echo_loads:
        load.start()

    barrier = pltpu.get_barrier_semaphore()
    pl.semaphore_signal(
        barrier, inc=1, device_id={"elev": other}, device_id_type=MESH
    )
    for route in ROUTES[:-1]:
        pl.semaphore_signal(
            barrier, inc=1, device_id={"ping": target_of(ping, route)}, device_id_type=MESH
        )

    @pl.when(ping < DIRECT)
    def _():
        for route in ROUTES[:-1]:
            pl.semaphore_signal(
                barrier, inc=1, device_id_type=MESH,
                device_id={"ping": target_of(ping, route), "elev": other},
            )

    @pl.when(rng < groups - 1)
    def _():
        for route in ROUTES:
            pl.semaphore_signal(
                barrier, inc=1, device_id_type=MESH,
                device_id={"ping": target_of(ping, route), "range": rng + 1},
            )

    @pl.when((rng < groups - 1) & (ping < DIRECT))
    def _():
        for route in ROUTES:
            pl.semaphore_signal(
                barrier, inc=1, device_id_type=MESH,
                device_id={"ping": target_of(ping, route), "range": rng + 1, "elev": other},
            )

    for load in loads:
        load.wait()
    for p in range(pings):
        line = jnp.broadcast_to(delay[p : p + 1, :], (2 * along, 2 * bins))
        turned = pltpu.roll(line, 0, 1, stride=1, stride_axis=0)
        table[p] = turned[:, bins:].astype(F32)
    for p in range(pings):
        valid = ap[p : p + 1, :] != 0
        picked = table[p, pl.ds(off[p], along), :]
        pick_t[pl.ds(p * along, along), :] = jnp.where(valid, picked, -1.0)
    picked = pick_t[...].T.astype(BF16)
    columns = picked.shape[0]
    one, zero = jnp.ones((), BF16), jnp.zeros((), BF16)
    starts = [sum(PARTS[:i]) for i in range(len(PARTS))]
    for start, some in zip(starts, PARTS):
        here = picked[start : start + some]
        for high in range(2):
            for low in range(4):
                weight[
                    pl.ds(2 * start + high * some, some), pl.ds(low * depth, depth)
                ] = jnp.where(here == 4 * high + low, one, zero)

    wide[...] = jnp.zeros_like(wide)
    lane = lanes((beams, bins))
    row = lax.broadcasted_iota(jnp.int32, (beams, bins), 0)
    for e in range(elems):
        rows = steer[e].astype(F32)
        for b in range(beams):
            spread[b, e] = jnp.broadcast_to(rows[b : b + 1], (8, bins))
        moved = pltpu.roll(jnp.where(lane < 8, rows, 0.0), 8, 1, stride=16, stride_axis=0)
        line = jnp.sum(moved, axis=0, keepdims=True)
        diag = jnp.where(lane % 16 - 8 == row, line, 0.0)
        diag = jnp.concatenate([diag, jnp.zeros_like(diag)], axis=0)
        wide[pl.ds(e * bins, 16), :] = diag.astype(BF16)

    def later(values, count):
        moved = pltpu.roll(values, bins - count, 1)
        return jnp.where(lanes(values.shape) < bins - count, moved, jnp.zeros((), values.dtype))

    def beam_rows(p, b):
        total = None
        for e in range(elems):
            line = jnp.concatenate([spread[b, e]] * (along // 8), axis=0)
            term = echo[p, e].astype(F32) * line
            total = term if total is None else total + term
        return total.astype(BF16)

    beam_parts = [[] for _ in range(beams)]
    for i, load in enumerate(echo_loads):
        load.wait()
        for b in range(beams):
            beam_parts[b] += [beam_rows(p, b) for p in range(i * each, (i + 1) * each)]

    store = {}

    class Put:
        def __init__(self, key):
            self.key = key

        def __setitem__(self, _, value):
            store[self.key] = value

    def RHS(b, low):
        return Put((b, low))

    def PAIR(q):
        return jnp.concatenate([jnp.concatenate([store[2*q,l] for l in range(4)],axis=0), jnp.concatenate([store[2*q+1,l] for l in range(4)],axis=0)],axis=1)

    def HEADS():
        return jnp.concatenate([store[beams,l] for l in range(4)],axis=0)

    flat = [jnp.concatenate([echo[p, e] for e in range(elems)], axis=1) for p in range(pings)]
    flat = jnp.concatenate(flat, axis=0)

    def make_heads():
        heads = jnp.dot(flat, wide[...], preferred_element_type=F32).astype(BF16)
        for low in range(4):
            moved = pltpu.roll(heads, bins - low, 1) if low else heads
            RHS(beams, low)[...] = moved

    def make_beam(b):
        beam = jnp.concatenate(beam_parts[b], axis=0)
        RHS(b, 0)[...] = beam
        for low in range(1, 4):
            RHS(b, low)[...] = later(beam, low)

    def project(start, some, b):
        picks = weight[pl.ds(2 * start, 2 * some), :]
        prod = jnp.dot(picks, PAIR(b // 2), preferred_element_type=F32)
        images = [
            prod[:some, c * bins : (c + 1) * bins]
            + later(prod[some:, c * bins : (c + 1) * bins], 4)
            for c in range(2)
        ]
        for j in range(some // 8):
            rows = [image[8 * j : 8 * j + 8] for image in images]
            stage[start // 16 + j // 2, j % 2, pl.ds(8 * b, 16), :] = jnp.concatenate(rows, axis=0).astype(BF16)

    def project_edge(start, some):
        picks = weight[pl.ds(2 * start, 2 * some), :]
        prod = jnp.dot(picks, HEADS(), preferred_element_type=F32)
        edge = prod[:some] + pltpu.roll(prod[some:], bins - 4, 1)
        for i in range(some // 16):
            for c in range(2):
                rows = edge[16 * i + 8 * c : 16 * i + 8 * c + 8]
                rows = jnp.concatenate([rows, jnp.zeros_like(rows)], axis=0).astype(BF16)
                stage[start // 16 + i, c, pl.ds(8 * beams, 16), :] = rows

    rest = pl.ds(DIRECT, ranks - DIRECT)
    swap = pltpu.make_async_remote_copy(
        src_ref=stage.at[rest, other],
        dst_ref=swapped.at[rest],
        send_sem=swap_send,
        recv_sem=swap_recv,
        device_id={"elev": other},
        device_id_type=MESH,
    )

    def share(source, slot, target, core):
        return pltpu.make_async_remote_copy(
            src_ref=source.at[pl.ds(0, 8 * beams)],
            dst_ref=got.at[slot],
            send_sem=share_send,
            recv_sem=share_recv,
            device_id={"ping": jnp.int32(target), "elev": core},
            device_id_type=MESH,
        )

    def spill(source, slot, target, core):
        return pltpu.make_async_remote_copy(
            src_ref=source.at[pl.ds(8 * beams, 16)],
            dst_ref=got_edge.at[slot],
            send_sem=edge_send,
            recv_sem=edge_recv,
            device_id={"ping": jnp.int32(target), "range": rng - 1, "elev": core},
            device_id_type=MESH,
        )

    def send_direct():
        slot = 2 * ping + elev
        for target in range(DIRECT):
            share(stage.at[target, other], slot, target, other).start()
            pl.when(ping != target)(share(stage.at[target, elev], slot, target, elev).start)

        @pl.when(rng > 0)
        def _():
            for target in range(DIRECT):
                for core in sides:
                    spill(stage.at[target, core], slot, target, core).start()

    def send_summed():
        for target in range(DIRECT):
            summed[target] = stage[target, elev]
        for target in range(DIRECT, ranks):
            both = stage[target, elev].astype(F32) + swapped[target].astype(F32)
            summed[target] = both.astype(BF16)
        for target in range(DIRECT, ranks):
            pl.when(ping != target)(share(summed.at[target], ping, target, elev).start)

        @pl.when(rng > 0)
        def _():
            for target in range(DIRECT, ranks):
                spill(summed.at[target], ping, target, elev).start()

    make_heads()
    for b in range(beams):
        make_beam(b)
    for b in range(0, beams, 2):
        project(0, columns, b)
    project_edge(0, columns)
    pl.semaphore_wait(
        barrier,
        ranks - 1 + DIRECT + jnp.where(ping < DIRECT, 0, 1) + jnp.where(rng > 0, ranks + DIRECT, 0),
    )
    swap.start()
    send_direct()
    swap.wait_recv()
    send_summed()

    def shares_of(count):
        return pltpu.make_async_remote_copy(
            src_ref=got.at[pl.ds(0, count)],
            dst_ref=got.at[pl.ds(0, count)],
            send_sem=share_send,
            recv_sem=share_recv,
            device_id={"elev": other},
            device_id_type=MESH,
        )

    def spills_of(count):
        return pltpu.make_async_remote_copy(
            src_ref=got_edge.at[pl.ds(0, count)],
            dst_ref=got_edge.at[pl.ds(0, count)],
            send_sem=edge_send,
            recv_sem=edge_recv,
            device_id={"elev": other},
            device_id_type=MESH,
        )

    direct = ping < DIRECT
    pl.when((rng < groups - 1) & direct)(spills_of(2 * ranks).wait_recv)
    pl.when((rng < groups - 1) & (ping >= DIRECT))(spills_of(ranks).wait_recv)

    @pl.when(rng == groups - 1)
    def _():
        got_edge[...] = jnp.zeros_like(got_edge)

    edge = jnp.zeros((16, bins), F32)
    for i in range(2 * ranks):
        part = got_edge[i].astype(F32)
        edge = edge + (part if i < ranks else jnp.where(direct, part, 0.0))
    edge = edge[:8]
    got[jnp.where(direct, 2 * ping + elev, ping)] = summed[ping, pl.ds(0, 8 * beams), :]
    pl.when(direct)(shares_of(2 * ranks - 1).wait_recv)
    pl.when(ping >= DIRECT)(shares_of(ranks - 1).wait_recv)
    total = jnp.zeros((beams * 8, bins), F32)
    for i in range(2 * ranks):
        part = got[i].astype(F32)
        total = total + (part if i < ranks else jnp.where(direct, part, 0.0))
    for b in range(beams):
        moved = pltpu.roll(edge, (2 * bins - 8 - 16 * b) % bins, 1)
        end = jnp.where(lane >= bins - 8, moved, 0.0)
        result[:, b, :] = (total[8 * b : 8 * b + 8] + end) * scale
    out_ref[...] = result[...].astype(BF16)

    shares_of(ranks - 1 + DIRECT).wait_send()
    swap.wait_send()
    pl.when(rng > 0)(spills_of(ranks + DIRECT).wait_send)


def solution(mesh):
    groups = mesh.shape["range"]
    ranks = mesh.shape["ping"]

    def body(echoes, steer, offsets, delays, aperture):
        pings, elems, along, bins = echoes.shape
        beams = steer.shape[1]
        columns = aperture.shape[0]
        depth = pings * along
        scale = float(ranks * pings * along) ** (-0.5)
        operands = (echoes, steer, offsets, delays, jnp.transpose(aperture))
        operands = [pltpu.with_memory_space_constraint(v, pltpu.HBM) for v in operands]
        return pl.pallas_call(
            functools.partial(kernel, scale, groups, ranks),
            out_shape=jax.ShapeDtypeStruct((8, beams, bins), BF16),
            in_specs=[pl.BlockSpec(memory_space=pltpu.HBM)] * 5,
            out_specs=pl.BlockSpec(memory_space=pltpu.VMEM),
            scratch_shapes=[
                pltpu.VMEM(echoes.shape, BF16),
                pltpu.VMEM(steer.shape, BF16),
                pltpu.SMEM(offsets.shape, jnp.int32),
                pltpu.VMEM(delays.shape, jnp.int32),
                pltpu.VMEM((pings, columns), jnp.int32),
                pltpu.VMEM((beams, elems, 8, bins), F32),
                pltpu.VMEM((pings, 2 * along, bins), F32),
                pltpu.VMEM((depth, columns), F32),
                pltpu.VMEM((2 * columns, 4 * depth), BF16),
                pltpu.VMEM((elems * bins, bins), BF16),
                pltpu.VMEM((4 * depth, (beams + 1) * bins), BF16),
                pltpu.VMEM((8, beams, bins), F32),
                pltpu.VMEM((ranks, 2, beams * 8 + 16, bins), BF16),
                pltpu.VMEM((ranks, beams * 8 + 16, bins), BF16),
                pltpu.VMEM((ranks, beams * 8 + 16, bins), BF16),
                pltpu.VMEM((2 * ranks, beams * 8, bins), BF16),
                pltpu.VMEM((2 * ranks, 16, bins), BF16),
                pltpu.SemaphoreType.DMA((6,)),
                pltpu.SemaphoreType.DMA,
                pltpu.SemaphoreType.DMA,
                pltpu.SemaphoreType.DMA,
                pltpu.SemaphoreType.DMA,
                pltpu.SemaphoreType.DMA,
                pltpu.SemaphoreType.DMA,
            ],
            compiler_params=pltpu.CompilerParams(
                collective_id=0, has_side_effects=True, vmem_limit_bytes=40 * 2**20
            ),
            cost_estimate=pl.CostEstimate(
                flops=2 * columns * DMAX * depth * beams * bins,
                bytes_accessed=echoes.size * 2,
                transcendentals=0,
            ),
        )(*operands)

    placed = (
        P("ping", "elev", None, "range"),
        P("elev", None, "range"),
        P("ping"),
        P("ping", None),
        P(None, "ping"),
    )
    return jax.shard_map(
        body,
        mesh=mesh,
        in_specs=placed,
        out_specs=P(("ping", "elev"), None, "range"),
        check_vma=False,
    )
```

```python
import functools

import jax
import jax.numpy as jnp
from jax import lax
from jax.experimental import pallas as pl
from jax.experimental.pallas import tpu as pltpu
from jax.sharding import PartitionSpec as P

MESH = pl.DeviceIdType.MESH
DMAX = 8
DIRECT = 3
PARTS = (128,)
F32 = jnp.float32
BF16 = jnp.bfloat16

ROUTES = ((2, 1), (2, 0), (1, 1), (3, 1), (0, 1), (1, 0), (3, 0), (0, 0))


def target_of(ping, route):
    steps, flip = route
    y, far = ping // 2, ping % 2
    return ((y + steps) % 4) * 2 + (far + flip) % 2


def lanes(shape):
    return lax.broadcasted_iota(jnp.int32, shape, len(shape) - 1)


def kernel(
    scale, groups, ranks,
    echo_hbm, steer_hbm, off_hbm, delay_hbm, ap_hbm, out_ref,
    echo, steer, off, delay, ap, spread, table, pick_t, weight, wide, rhs, result,
    stage, swapped, summed, got, got_edge,
    small_sem, share_send, share_recv, edge_send, edge_recv, swap_send, swap_recv,
):
    ping = lax.axis_index("ping")
    rng = lax.axis_index("range")
    elev = lax.axis_index("elev")
    other = 1 - elev
    sides = (other, elev)
    pings, elems, along, bins = echo.shape
    beams = steer.shape[1]
    depth = pings * along

    barrier = pltpu.get_barrier_semaphore()
    pl.semaphore_signal(
        barrier, inc=1, device_id={"elev": other}, device_id_type=MESH
    )
    for route in ROUTES[:-1]:
        pl.semaphore_signal(
            barrier, inc=1, device_id={"ping": target_of(ping, route)}, device_id_type=MESH
        )

    @pl.when(ping < DIRECT)
    def _():
        for route in ROUTES[:-1]:
            pl.semaphore_signal(
                barrier, inc=1, device_id_type=MESH,
                device_id={"ping": target_of(ping, route), "elev": other},
            )

    @pl.when(rng < groups - 1)
    def _():
        for route in ROUTES:
            pl.semaphore_signal(
                barrier, inc=1, device_id_type=MESH,
                device_id={"ping": target_of(ping, route), "range": rng + 1},
            )

    @pl.when((rng < groups - 1) & (ping < DIRECT))
    def _():
        for route in ROUTES:
            pl.semaphore_signal(
                barrier, inc=1, device_id_type=MESH,
                device_id={"ping": target_of(ping, route), "range": rng + 1, "elev": other},
            )

    loads = [
        pltpu.make_async_copy(src, dst, small_sem.at[i])
        for i, (src, dst) in enumerate(
            ((steer_hbm, steer), (delay_hbm, delay), (off_hbm, off), (ap_hbm, ap))
        )
    ]
    for load in loads:
        load.start()
    each = pings // 2
    echo_loads = [
        pltpu.make_async_copy(
            echo_hbm.at[pl.ds(i * each, each)], echo.at[pl.ds(i * each, each)], small_sem.at[4 + i]
        )
        for i in range(2)
    ]
    for load in echo_loads:
        load.start()

    for load in loads:
        load.wait()
    for p in range(pings):
        line = jnp.broadcast_to(delay[p : p + 1, :], (2 * along, 2 * bins))
        turned = pltpu.roll(line, 0, 1, stride=1, stride_axis=0)
        table[p] = turned[:, bins:].astype(F32)
    for p in range(pings):
        valid = ap[p : p + 1, :] != 0
        picked = table[p, pl.ds(off[p], along), :]
        pick_t[pl.ds(p * along, along), :] = jnp.where(valid, picked, -1.0)
    picked = pick_t[...].T.astype(BF16)
    columns = picked.shape[0]
    one, zero = jnp.ones((), BF16), jnp.zeros((), BF16)
    starts = [sum(PARTS[:i]) for i in range(len(PARTS))]
    for start, some in zip(starts, PARTS):
        here = picked[start : start + some]
        for high in range(2):
            for low in range(4):
                weight[
                    pl.ds(2 * start + high * some, some), pl.ds(low * depth, depth)
                ] = jnp.where(here == 4 * high + low, one, zero)

    wide[...] = jnp.zeros_like(wide)
    lane = lanes((beams, bins))
    row = lax.broadcasted_iota(jnp.int32, (beams, bins), 0)
    for e in range(elems):
        rows = steer[e].astype(F32)
        for b in range(beams):
            spread[b, e] = jnp.broadcast_to(rows[b : b + 1], (8, bins))
        moved = pltpu.roll(jnp.where(lane < 8, rows, 0.0), 8, 1, stride=16, stride_axis=0)
        line = jnp.sum(moved, axis=0, keepdims=True)
        diag = jnp.where(lane % 16 - 8 == row, line, 0.0)
        diag = jnp.concatenate([diag, jnp.zeros_like(diag)], axis=0)
        wide[pl.ds(e * bins, 16), :] = diag.astype(BF16)

    def later(values, count):
        moved = pltpu.roll(values, bins - count, 1)
        return jnp.where(lanes(values.shape) < bins - count, moved, jnp.zeros((), values.dtype))

    def beam_rows(p, b):
        total = None
        for e in range(elems):
            line = jnp.concatenate([spread[b, e]] * (along // 8), axis=0)
            term = echo[p, e].astype(F32) * line
            total = term if total is None else total + term
        return total.astype(BF16)

    beam_parts = [[] for _ in range(beams)]
    for i, load in enumerate(echo_loads):
        load.wait()
        for b in range(beams):
            beam_parts[b] += [beam_rows(p, b) for p in range(i * each, (i + 1) * each)]

    store = {}

    class Put:
        def __init__(self, key):
            self.key = key

        def __setitem__(self, _, value):
            store[self.key] = value

    def RHS(b, low):
        return Put((b, low))

    def PAIR(q):
        return jnp.concatenate([jnp.concatenate([store[2*q,l] for l in range(4)],axis=0), jnp.concatenate([store[2*q+1,l] for l in range(4)],axis=0)],axis=1)

    def HEADS():
        return jnp.concatenate([store[beams,l] for l in range(4)],axis=0)

    flat = [jnp.concatenate([echo[p, e] for e in range(elems)], axis=1) for p in range(pings)]
    flat = jnp.concatenate(flat, axis=0)

    def make_heads():
        heads = jnp.dot(flat, wide[...], preferred_element_type=F32).astype(BF16)
        for low in range(4):
            moved = pltpu.roll(heads, bins - low, 1) if low else heads
            RHS(beams, low)[...] = moved

    def make_beam(b):
        beam = jnp.concatenate(beam_parts[b], axis=0)
        RHS(b, 0)[...] = beam
        for low in range(1, 4):
            RHS(b, low)[...] = later(beam, low)

    def project(start, some, b):
        picks = weight[pl.ds(2 * start, 2 * some), :]
        prod = jnp.dot(picks, PAIR(b // 2), preferred_element_type=F32)
        images = [
            prod[:some, c * bins : (c + 1) * bins]
            + later(prod[some:, c * bins : (c + 1) * bins], 4)
            for c in range(2)
        ]
        for j in range(some // 8):
            rows = [image[8 * j : 8 * j + 8] for image in images]
            stage[start // 16 + j // 2, j % 2, pl.ds(8 * b, 16), :] = jnp.concatenate(rows, axis=0).astype(BF16)

    def project_edge(start, some):
        picks = weight[pl.ds(2 * start, 2 * some), :]
        prod = jnp.dot(picks, HEADS(), preferred_element_type=F32)
        edge = prod[:some] + pltpu.roll(prod[some:], bins - 4, 1)
        for i in range(some // 16):
            for c in range(2):
                rows = edge[16 * i + 8 * c : 16 * i + 8 * c + 8]
                rows = jnp.concatenate([rows, jnp.zeros_like(rows)], axis=0).astype(BF16)
                stage[start // 16 + i, c, pl.ds(8 * beams, 16), :] = rows

    rest = pl.ds(DIRECT, ranks - DIRECT)
    swap = pltpu.make_async_remote_copy(
        src_ref=stage.at[rest, other],
        dst_ref=swapped.at[rest],
        send_sem=swap_send,
        recv_sem=swap_recv,
        device_id={"elev": other},
        device_id_type=MESH,
    )

    def share(source, slot, target, core):
        return pltpu.make_async_remote_copy(
            src_ref=source.at[pl.ds(0, 8 * beams)],
            dst_ref=got.at[slot],
            send_sem=share_send,
            recv_sem=share_recv,
            device_id={"ping": jnp.int32(target), "elev": core},
            device_id_type=MESH,
        )

    def spill(source, slot, target, core):
        return pltpu.make_async_remote_copy(
            src_ref=source.at[pl.ds(8 * beams, 16)],
            dst_ref=got_edge.at[slot],
            send_sem=edge_send,
            recv_sem=edge_recv,
            device_id={"ping": jnp.int32(target), "range": rng - 1, "elev": core},
            device_id_type=MESH,
        )

    def send_direct():
        slot = 2 * ping + elev
        for target in range(DIRECT):
            share(stage.at[target, other], slot, target, other).start()
            pl.when(ping != target)(share(stage.at[target, elev], slot, target, elev).start)

        @pl.when(rng > 0)
        def _():
            for target in range(DIRECT):
                for core in sides:
                    spill(stage.at[target, core], slot, target, core).start()

    def send_summed():
        for target in range(DIRECT):
            summed[target] = stage[target, elev]
        for target in range(DIRECT, ranks):
            both = stage[target, elev].astype(F32) + swapped[target].astype(F32)
            summed[target] = both.astype(BF16)
        for target in range(DIRECT, ranks):
            pl.when(ping != target)(share(summed.at[target], ping, target, elev).start)

        @pl.when(rng > 0)
        def _():
            for target in range(DIRECT, ranks):
                spill(summed.at[target], ping, target, elev).start()

    make_heads()
    for b in range(beams):
        make_beam(b)
    for b in range(0, beams, 2):
        project(0, columns, b)
    project_edge(0, columns)
    pl.semaphore_wait(
        barrier,
        ranks - 1 + DIRECT + jnp.where(ping < DIRECT, 0, 1) + jnp.where(rng > 0, ranks + DIRECT, 0),
    )
    swap.start()
    send_direct()
    swap.wait_recv()
    send_summed()

    def shares_of(count):
        return pltpu.make_async_remote_copy(
            src_ref=got.at[pl.ds(0, count)],
            dst_ref=got.at[pl.ds(0, count)],
            send_sem=share_send,
            recv_sem=share_recv,
            device_id={"elev": other},
            device_id_type=MESH,
        )

    def spills_of(count):
        return pltpu.make_async_remote_copy(
            src_ref=got_edge.at[pl.ds(0, count)],
            dst_ref=got_edge.at[pl.ds(0, count)],
            send_sem=edge_send,
            recv_sem=edge_recv,
            device_id={"elev": other},
            device_id_type=MESH,
        )

    direct = ping < DIRECT
    pl.when((rng < groups - 1) & direct)(spills_of(2 * ranks).wait_recv)
    pl.when((rng < groups - 1) & (ping >= DIRECT))(spills_of(ranks).wait_recv)

    @pl.when(rng == groups - 1)
    def _():
        got_edge[...] = jnp.zeros_like(got_edge)

    edge = jnp.zeros((16, bins), F32)
    for i in range(2 * ranks):
        part = got_edge[i].astype(F32)
        edge = edge + (part if i < ranks else jnp.where(direct, part, 0.0))
    edge = edge[:8]
    got[jnp.where(direct, 2 * ping + elev, ping)] = summed[ping, pl.ds(0, 8 * beams), :]
    pl.when(direct)(shares_of(2 * ranks - 1).wait_recv)
    pl.when(ping >= DIRECT)(shares_of(ranks - 1).wait_recv)
    total = jnp.zeros((beams * 8, bins), F32)
    for i in range(2 * ranks):
        part = got[i].astype(F32)
        total = total + (part if i < ranks else jnp.where(direct, part, 0.0))
    for b in range(beams):
        moved = pltpu.roll(edge, (2 * bins - 8 - 16 * b) % bins, 1)
        end = jnp.where(lane >= bins - 8, moved, 0.0)
        result[:, b, :] = (total[8 * b : 8 * b + 8] + end) * scale
    out_ref[...] = result[...].astype(BF16)

    shares_of(ranks - 1 + DIRECT).wait_send()
    swap.wait_send()
    pl.when(rng > 0)(spills_of(ranks + DIRECT).wait_send)


def solution(mesh):
    groups = mesh.shape["range"]
    ranks = mesh.shape["ping"]

    def body(echoes, steer, offsets, delays, aperture):
        pings, elems, along, bins = echoes.shape
        beams = steer.shape[1]
        columns = aperture.shape[0]
        depth = pings * along
        scale = float(ranks * pings * along) ** (-0.5)
        operands = (echoes, steer, offsets, delays, jnp.transpose(aperture))
        operands = [pltpu.with_memory_space_constraint(v, pltpu.HBM) for v in operands]
        return pl.pallas_call(
            functools.partial(kernel, scale, groups, ranks),
            out_shape=jax.ShapeDtypeStruct((8, beams, bins), BF16),
            in_specs=[pl.BlockSpec(memory_space=pltpu.HBM)] * 5,
            out_specs=pl.BlockSpec(memory_space=pltpu.VMEM),
            scratch_shapes=[
                pltpu.VMEM(echoes.shape, BF16),
                pltpu.VMEM(steer.shape, BF16),
                pltpu.SMEM(offsets.shape, jnp.int32),
                pltpu.VMEM(delays.shape, jnp.int32),
                pltpu.VMEM((pings, columns), jnp.int32),
                pltpu.VMEM((beams, elems, 8, bins), F32),
                pltpu.VMEM((pings, 2 * along, bins), F32),
                pltpu.VMEM((depth, columns), F32),
                pltpu.VMEM((2 * columns, 4 * depth), BF16),
                pltpu.VMEM((elems * bins, bins), BF16),
                pltpu.VMEM((4 * depth, (beams + 1) * bins), BF16),
                pltpu.VMEM((8, beams, bins), F32),
                pltpu.VMEM((ranks, 2, beams * 8 + 16, bins), BF16),
                pltpu.VMEM((ranks, beams * 8 + 16, bins), BF16),
                pltpu.VMEM((ranks, beams * 8 + 16, bins), BF16),
                pltpu.VMEM((2 * ranks, beams * 8, bins), BF16),
                pltpu.VMEM((2 * ranks, 16, bins), BF16),
                pltpu.SemaphoreType.DMA((6,)),
                pltpu.SemaphoreType.DMA,
                pltpu.SemaphoreType.DMA,
                pltpu.SemaphoreType.DMA,
                pltpu.SemaphoreType.DMA,
                pltpu.SemaphoreType.DMA,
                pltpu.SemaphoreType.DMA,
            ],
            compiler_params=pltpu.CompilerParams(
                collective_id=0, has_side_effects=True, vmem_limit_bytes=40 * 2**20
            ),
            cost_estimate=pl.CostEstimate(
                flops=2 * columns * DMAX * depth * beams * bins,
                bytes_accessed=echoes.size * 2,
                transcendentals=0,
            ),
        )(*operands)

    placed = (
        P("ping", "elev", None, "range"),
        P("elev", None, "range"),
        P("ping"),
        P("ping", None),
        P(None, "ping"),
    )
    return jax.shard_map(
        body,
        mesh=mesh,
        in_specs=placed,
        out_specs=P(("ping", "elev"), None, "range"),
        check_vma=False,
    )
```

```python
import functools

import jax
import jax.numpy as jnp
from jax import lax
from jax.experimental import pallas as pl
from jax.experimental.pallas import tpu as pltpu
from jax.sharding import PartitionSpec as P

MESH = pl.DeviceIdType.MESH
DMAX = 8
DIRECT = 3
PARTS = (128,)
F32 = jnp.float32
BF16 = jnp.bfloat16

ROUTES = ((2, 1), (2, 0), (1, 1), (3, 1), (0, 1), (1, 0), (3, 0), (0, 0))


def target_of(ping, route):
    steps, flip = route
    y, far = ping // 2, ping % 2
    return ((y + steps) % 4) * 2 + (far + flip) % 2


def lanes(shape):
    return lax.broadcasted_iota(jnp.int32, shape, len(shape) - 1)


def kernel(
    scale, groups, ranks,
    echo_hbm, steer_hbm, off_hbm, delay_hbm, ap_hbm, out_ref,
    echo, steer, off, delay, ap, spread, table, pick_t, weight, wide, rhs, result,
    stage, swapped, summed, got, got_edge,
    small_sem, share_send, share_recv, edge_send, edge_recv, swap_send, swap_recv,
):
    ping = lax.axis_index("ping")
    rng = lax.axis_index("range")
    elev = lax.axis_index("elev")
    other = 1 - elev
    sides = (other, elev)
    pings, elems, along, bins = echo.shape
    beams = steer.shape[1]
    depth = pings * along

    barrier = pltpu.get_barrier_semaphore()
    pl.semaphore_signal(
        barrier, inc=1, device_id={"elev": other}, device_id_type=MESH
    )
    for route in ROUTES[:-1]:
        pl.semaphore_signal(
            barrier, inc=1, device_id={"ping": target_of(ping, route)}, device_id_type=MESH
        )

    @pl.when(ping < DIRECT)
    def _():
        for route in ROUTES[:-1]:
            pl.semaphore_signal(
                barrier, inc=1, device_id_type=MESH,
                device_id={"ping": target_of(ping, route), "elev": other},
            )

    @pl.when(rng < groups - 1)
    def _():
        for route in ROUTES:
            pl.semaphore_signal(
                barrier, inc=1, device_id_type=MESH,
                device_id={"ping": target_of(ping, route), "range": rng + 1},
            )

    @pl.when((rng < groups - 1) & (ping < DIRECT))
    def _():
        for route in ROUTES:
            pl.semaphore_signal(
                barrier, inc=1, device_id_type=MESH,
                device_id={"ping": target_of(ping, route), "range": rng + 1, "elev": other},
            )

    loads = [
        pltpu.make_async_copy(src, dst, small_sem.at[i])
        for i, (src, dst) in enumerate(
            ((steer_hbm, steer), (delay_hbm, delay), (off_hbm, off), (ap_hbm, ap))
        )
    ]
    each = pings // 2
    echo_loads = [
        pltpu.make_async_copy(
            echo_hbm.at[pl.ds(i * each, each)], echo.at[pl.ds(i * each, each)], small_sem.at[4 + i]
        )
        for i in range(2)
    ]
    for load in echo_loads:
        load.start()
    for load in loads:
        load.start()

    for load in loads:
        load.wait()
    for p in range(pings):
        line = jnp.broadcast_to(delay[p : p + 1, :], (2 * along, 2 * bins))
        turned = pltpu.roll(line, 0, 1, stride=1, stride_axis=0)
        table[p] = turned[:, bins:].astype(F32)
    for p in range(pings):
        valid = ap[p : p + 1, :] != 0
        picked = table[p, pl.ds(off[p], along), :]
        pick_t[pl.ds(p * along, along), :] = jnp.where(valid, picked, -1.0)
    picked = pick_t[...].T.astype(BF16)
    columns = picked.shape[0]
    one, zero = jnp.ones((), BF16), jnp.zeros((), BF16)
    starts = [sum(PARTS[:i]) for i in range(len(PARTS))]
    for start, some in zip(starts, PARTS):
        here = picked[start : start + some]
        for high in range(2):
            for low in range(4):
                weight[
                    pl.ds(2 * start + high * some, some), pl.ds(low * depth, depth)
                ] = jnp.where(here == 4 * high + low, one, zero)

    wide[...] = jnp.zeros_like(wide)
    lane = lanes((beams, bins))
    row = lax.broadcasted_iota(jnp.int32, (beams, bins), 0)
    for e in range(elems):
        rows = steer[e].astype(F32)
        for b in range(beams):
            spread[b, e] = jnp.broadcast_to(rows[b : b + 1], (8, bins))
        moved = pltpu.roll(jnp.where(lane < 8, rows, 0.0), 8, 1, stride=16, stride_axis=0)
        line = jnp.sum(moved, axis=0, keepdims=True)
        diag = jnp.where(lane % 16 - 8 == row, line, 0.0)
        diag = jnp.concatenate([diag, jnp.zeros_like(diag)], axis=0)
        wide[pl.ds(e * bins, 16), :] = diag.astype(BF16)

    def later(values, count):
        moved = pltpu.roll(values, bins - count, 1)
        return jnp.where(lanes(values.shape) < bins - count, moved, jnp.zeros((), values.dtype))

    def beam_rows(p, b):
        total = None
        for e in range(elems):
            line = jnp.concatenate([spread[b, e]] * (along // 8), axis=0)
            term = echo[p, e].astype(F32) * line
            total = term if total is None else total + term
        return total.astype(BF16)

    beam_parts = [[] for _ in range(beams)]
    for i, load in enumerate(echo_loads):
        load.wait()
        for b in range(beams):
            beam_parts[b] += [beam_rows(p, b) for p in range(i * each, (i + 1) * each)]

    store = {}

    class Put:
        def __init__(self, key):
            self.key = key

        def __setitem__(self, _, value):
            store[self.key] = value

    def RHS(b, low):
        return Put((b, low))

    def PAIR(q):
        return jnp.concatenate([jnp.concatenate([store[2*q,l] for l in range(4)],axis=0), jnp.concatenate([store[2*q+1,l] for l in range(4)],axis=0)],axis=1)

    def HEADS():
        return jnp.concatenate([store[beams,l] for l in range(4)],axis=0)

    flat = [jnp.concatenate([echo[p, e] for e in range(elems)], axis=1) for p in range(pings)]
    flat = jnp.concatenate(flat, axis=0)

    def make_heads():
        heads = jnp.dot(flat, wide[...], preferred_element_type=F32).astype(BF16)
        for low in range(4):
            moved = pltpu.roll(heads, bins - low, 1) if low else heads
            RHS(beams, low)[...] = moved

    def make_beam(b):
        beam = jnp.concatenate(beam_parts[b], axis=0)
        RHS(b, 0)[...] = beam
        for low in range(1, 4):
            RHS(b, low)[...] = later(beam, low)

    def project(start, some, b):
        picks = weight[pl.ds(2 * start, 2 * some), :]
        prod = jnp.dot(picks, PAIR(b // 2), preferred_element_type=F32)
        images = [
            prod[:some, c * bins : (c + 1) * bins]
            + later(prod[some:, c * bins : (c + 1) * bins], 4)
            for c in range(2)
        ]
        for j in range(some // 8):
            rows = [image[8 * j : 8 * j + 8] for image in images]
            stage[start // 16 + j // 2, j % 2, pl.ds(8 * b, 16), :] = jnp.concatenate(rows, axis=0).astype(BF16)

    def project_edge(start, some):
        picks = weight[pl.ds(2 * start, 2 * some), :]
        prod = jnp.dot(picks, HEADS(), preferred_element_type=F32)
        edge = prod[:some] + pltpu.roll(prod[some:], bins - 4, 1)
        for i in range(some // 16):
            for c in range(2):
                rows = edge[16 * i + 8 * c : 16 * i + 8 * c + 8]
                rows = jnp.concatenate([rows, jnp.zeros_like(rows)], axis=0).astype(BF16)
                stage[start // 16 + i, c, pl.ds(8 * beams, 16), :] = rows

    rest = pl.ds(DIRECT, ranks - DIRECT)
    swap = pltpu.make_async_remote_copy(
        src_ref=stage.at[rest, other],
        dst_ref=swapped.at[rest],
        send_sem=swap_send,
        recv_sem=swap_recv,
        device_id={"elev": other},
        device_id_type=MESH,
    )

    def share(source, slot, target, core):
        return pltpu.make_async_remote_copy(
            src_ref=source.at[pl.ds(0, 8 * beams)],
            dst_ref=got.at[slot],
            send_sem=share_send,
            recv_sem=share_recv,
            device_id={"ping": jnp.int32(target), "elev": core},
            device_id_type=MESH,
        )

    def spill(source, slot, target, core):
        return pltpu.make_async_remote_copy(
            src_ref=source.at[pl.ds(8 * beams, 16)],
            dst_ref=got_edge.at[slot],
            send_sem=edge_send,
            recv_sem=edge_recv,
            device_id={"ping": jnp.int32(target), "range": rng - 1, "elev": core},
            device_id_type=MESH,
        )

    def send_direct():
        slot = 2 * ping + elev
        for target in range(DIRECT):
            share(stage.at[target, other], slot, target, other).start()
            pl.when(ping != target)(share(stage.at[target, elev], slot, target, elev).start)

        @pl.when(rng > 0)
        def _():
            for target in range(DIRECT):
                for core in sides:
                    spill(stage.at[target, core], slot, target, core).start()

    def send_summed():
        for target in range(DIRECT):
            summed[target] = stage[target, elev]
        for target in range(DIRECT, ranks):
            both = stage[target, elev].astype(F32) + swapped[target].astype(F32)
            summed[target] = both.astype(BF16)
        for target in range(DIRECT, ranks):
            pl.when(ping != target)(share(summed.at[target], ping, target, elev).start)

        @pl.when(rng > 0)
        def _():
            for target in range(DIRECT, ranks):
                spill(summed.at[target], ping, target, elev).start()

    make_heads()
    for b in range(beams):
        make_beam(b)
    for b in range(0, beams, 2):
        project(0, columns, b)
    project_edge(0, columns)
    pl.semaphore_wait(
        barrier,
        ranks - 1 + DIRECT + jnp.where(ping < DIRECT, 0, 1) + jnp.where(rng > 0, ranks + DIRECT, 0),
    )
    swap.start()
    send_direct()
    swap.wait_recv()
    send_summed()

    def shares_of(count):
        return pltpu.make_async_remote_copy(
            src_ref=got.at[pl.ds(0, count)],
            dst_ref=got.at[pl.ds(0, count)],
            send_sem=share_send,
            recv_sem=share_recv,
            device_id={"elev": other},
            device_id_type=MESH,
        )

    def spills_of(count):
        return pltpu.make_async_remote_copy(
            src_ref=got_edge.at[pl.ds(0, count)],
            dst_ref=got_edge.at[pl.ds(0, count)],
            send_sem=edge_send,
            recv_sem=edge_recv,
            device_id={"elev": other},
            device_id_type=MESH,
        )

    direct = ping < DIRECT
    pl.when((rng < groups - 1) & direct)(spills_of(2 * ranks).wait_recv)
    pl.when((rng < groups - 1) & (ping >= DIRECT))(spills_of(ranks).wait_recv)

    @pl.when(rng == groups - 1)
    def _():
        got_edge[...] = jnp.zeros_like(got_edge)

    edge = jnp.zeros((16, bins), F32)
    for i in range(2 * ranks):
        part = got_edge[i].astype(F32)
        edge = edge + (part if i < ranks else jnp.where(direct, part, 0.0))
    edge = edge[:8]
    got[jnp.where(direct, 2 * ping + elev, ping)] = summed[ping, pl.ds(0, 8 * beams), :]
    pl.when(direct)(shares_of(2 * ranks - 1).wait_recv)
    pl.when(ping >= DIRECT)(shares_of(ranks - 1).wait_recv)
    total = jnp.zeros((beams * 8, bins), F32)
    for i in range(2 * ranks):
        part = got[i].astype(F32)
        total = total + (part if i < ranks else jnp.where(direct, part, 0.0))
    for b in range(beams):
        moved = pltpu.roll(edge, (2 * bins - 8 - 16 * b) % bins, 1)
        end = jnp.where(lane >= bins - 8, moved, 0.0)
        result[:, b, :] = (total[8 * b : 8 * b + 8] + end) * scale
    out_ref[...] = result[...].astype(BF16)

    shares_of(ranks - 1 + DIRECT).wait_send()
    swap.wait_send()
    pl.when(rng > 0)(spills_of(ranks + DIRECT).wait_send)


def solution(mesh):
    groups = mesh.shape["range"]
    ranks = mesh.shape["ping"]

    def body(echoes, steer, offsets, delays, aperture):
        pings, elems, along, bins = echoes.shape
        beams = steer.shape[1]
        columns = aperture.shape[0]
        depth = pings * along
        scale = float(ranks * pings * along) ** (-0.5)
        operands = (echoes, steer, offsets, delays, jnp.transpose(aperture))
        operands = [pltpu.with_memory_space_constraint(v, pltpu.HBM) for v in operands]
        return pl.pallas_call(
            functools.partial(kernel, scale, groups, ranks),
            out_shape=jax.ShapeDtypeStruct((8, beams, bins), BF16),
            in_specs=[pl.BlockSpec(memory_space=pltpu.HBM)] * 5,
            out_specs=pl.BlockSpec(memory_space=pltpu.VMEM),
            scratch_shapes=[
                pltpu.VMEM(echoes.shape, BF16),
                pltpu.VMEM(steer.shape, BF16),
                pltpu.SMEM(offsets.shape, jnp.int32),
                pltpu.VMEM(delays.shape, jnp.int32),
                pltpu.VMEM((pings, columns), jnp.int32),
                pltpu.VMEM((beams, elems, 8, bins), F32),
                pltpu.VMEM((pings, 2 * along, bins), F32),
                pltpu.VMEM((depth, columns), F32),
                pltpu.VMEM((2 * columns, 4 * depth), BF16),
                pltpu.VMEM((elems * bins, bins), BF16),
                pltpu.VMEM((4 * depth, (beams + 1) * bins), BF16),
                pltpu.VMEM((8, beams, bins), F32),
                pltpu.VMEM((ranks, 2, beams * 8 + 16, bins), BF16),
                pltpu.VMEM((ranks, beams * 8 + 16, bins), BF16),
                pltpu.VMEM((ranks, beams * 8 + 16, bins), BF16),
                pltpu.VMEM((2 * ranks, beams * 8, bins), BF16),
                pltpu.VMEM((2 * ranks, 16, bins), BF16),
                pltpu.SemaphoreType.DMA((6,)),
                pltpu.SemaphoreType.DMA,
                pltpu.SemaphoreType.DMA,
                pltpu.SemaphoreType.DMA,
                pltpu.SemaphoreType.DMA,
                pltpu.SemaphoreType.DMA,
                pltpu.SemaphoreType.DMA,
            ],
            compiler_params=pltpu.CompilerParams(
                collective_id=0, has_side_effects=True, vmem_limit_bytes=40 * 2**20
            ),
            cost_estimate=pl.CostEstimate(
                flops=2 * columns * DMAX * depth * beams * bins,
                bytes_accessed=echoes.size * 2,
                transcendentals=0,
            ),
        )(*operands)

    placed = (
        P("ping", "elev", None, "range"),
        P("elev", None, "range"),
        P("ping"),
        P("ping", None),
        P(None, "ping"),
    )
    return jax.shard_map(
        body,
        mesh=mesh,
        in_specs=placed,
        out_specs=P(("ping", "elev"), None, "range"),
        check_vma=False,
    )
```
